32 devices in a mesh: tm: 16 (over z, x, core), freq: 2 (over y).
Axes of the slice: x: 2, y: 2, z: 4, core: 2. Of those that a mesh axis runs over, the one named last changes fastest.
Arguments:
- visibilities: float32 [16, 2, 8, 512], P('tm', 'freq'), may hold values from -6 to 6
- coherency: bfloat16 [16, 2, 8, 64, 512], P('tm', 'freq'), may hold values from -0.75 to 0.75
- stations: int32 [16, 2, 512], P('tm'), may hold values from 0 to 511, as said below
- jones: float32 [2, 8, 32768], P('freq', None, 'tm'), may hold values from -3 to 3
- dual: float32 [2, 8, 32768], P('freq', None, 'tm'), may hold values from -1.8 to 1.8
- cluster: int32 [64], replicated, may hold values from 0 to 7
- rho_table: float32 [8], replicated, may hold values from 0.3 to 3
Outputs:
- jones_out: float32 [2, 8, 32768], P('freq', None, 'tm')
- dual_out: float32 [2, 8, 32768], P('freq', None, 'tm')
- consensus: float32 [1, 8, 32768], P(None, None, 'tm')
The draws below stay inside these ranges and needn't reach their ends.
Inputs may be any that keep to these rules, and one draw needn't show every extreme that they name: Each baseline joins two different stations.
All inputs are finite; a program needn't handle non-finite values.
Results may differ from the reference program's by a relative error of at most 0.0003.
Values may be sent and summed in bfloat16 or wider, within the bound.
A program may use at most 64 MiB of HBM per device.

```python
import math
import jax
import jax.numpy as jnp
import numpy as np
from jax import lax

S = 512
K = 64
NCL = 8
BL_DEV = 512
ITERS = 2
TIMES = 16
NCH = 2
NP = 1


def draw_stations(key, part):
    key_first, key_offset = jax.random.split(jax.random.fold_in(key, 11))
    first_st = jax.random.randint(key_first, (TIMES, BL_DEV), 0, S)
    offsets = jax.random.randint(key_offset, (TIMES, BL_DEV), 1, S)
    second_st = (first_st + offsets) % S
    leading = jnp.arange(BL_DEV)[None, :] == 0
    first_st = jnp.where(leading, 0, first_st)
    second_st = jnp.where(leading, S - 1, second_st)
    return jnp.stack([first_st, second_st], axis=1).astype(jnp.int32)


def draw_jones(key, part):
    inner_key = jax.random.fold_in(key, 23)
    direction = (jnp.arange(K * S) // S).astype(jnp.float32)
    spread = 0.4 + 0.8 * direction / (K - 1)
    values = jnp.clip(jax.random.normal(inner_key, (NCH, 8, K * S), jnp.float32), -2.5, 2.5)
    return (values * spread[None, None, :]).astype(jnp.float32)


def plant(values, rng, smallest, top_value):
    spot = [jax.random.randint(jax.random.fold_in(rng, axis), (), 0, length) for axis, length in enumerate(values.shape)]
    longest = values.shape.index(max(values.shape))
    neighbour = spot[:longest] + [(spot[longest] + 1) % values.shape[longest]] + spot[longest + 1:]
    return values.at[tuple(spot)].set(smallest).at[tuple(neighbour)].set(top_value)


def block_levels(key, shape, shards, low, top_value):
    def one(dim, parts):
        draws = jax.random.uniform(jax.random.fold_in(jax.random.fold_in(key, 6), dim), (parts,), jnp.float32, low / len(shards), top_value / len(shards))
        return jnp.repeat(jnp.exp(draws), shape[dim] // parts).reshape((-1,) + (1,) * (len(shape) - dim - 1))

    factor_of = one(*shards[0])
    for cut in shards[1:]:
        factor_of = factor_of * one(*cut)
    return factor_of


def scatter_about(own_key, shape, scale, most, pieces=(), kind=jnp.bfloat16):
    drawn = jax.random.normal(own_key, shape, jnp.float32) * scale
    if len(pieces) > 0:
        drawn = block_levels(own_key, shape, pieces, -0.22, 0.18) * drawn
    return jnp.clip(drawn, min=-most, max=most).astype(kind)


def setup_inputs(seed: int = 0) -> dict:
    streams_of = jax.random.split(jax.random.key(seed), 8)
    return {
        "visibilities": scatter_about(streams_of[0], (TIMES, NCH, 8, BL_DEV), 1.0, 6.0, ((0, 16), (1, 2)), jnp.float32),
        "coherency": scatter_about(streams_of[1], (TIMES, NCH, 8, K, BL_DEV), 0.125, 0.75, ((0, 16), (1, 2))),
        "stations": draw_stations(jax.random.fold_in(streams_of[7], 71), 0),
        "jones": draw_jones(jax.random.fold_in(streams_of[7], 71), 0),
        "dual": scatter_about(streams_of[4], (NCH, 8, K * S), 0.3, 1.8, ((0, 2), (2, 16)), jnp.float32),
        "cluster": plant(jax.random.randint(streams_of[5], (K,), 0, NCL), jax.random.fold_in(streams_of[5], 1), 0, NCL - 1).astype(jnp.int32),
        "rho_table": jnp.clip(jnp.exp(jax.random.uniform(streams_of[6], (NCL,), jnp.float32, math.log(0.3), math.log(3.0))), 0.3, 3.0),
    }


step_size = 0.5
epsilon = 1e-06
highest = lax.Precision.HIGHEST

def poly_basis(channels, degrees):
    points = np.linspace(-1.0, 1.0, channels)
    columns = []
    for degree in range(degrees):
        column = points ** degree
        for earlier in columns:
            column = column - np.dot(earlier, column) * earlier
        column = column / np.sqrt(np.dot(column, column))
        columns.append(column)
    return np.stack(columns, axis=1).astype(np.float32)

def split_entries(stacked):
    return [[(stacked[4 * left_index + 2 * right_index], stacked[4 * left_index + 2 * right_index + 1]) for right_index in range(2)] for left_index in range(2)]

def times_pair(left_val, right_val):
    return (left_val[0] * right_val[0] - left_val[1] * right_val[1], left_val[0] * right_val[1] + left_val[1] * right_val[0])

def times_conj(left_val, right_val):
    return (left_val[0] * right_val[0] + left_val[1] * right_val[1], left_val[1] * right_val[0] - left_val[0] * right_val[1])

def add_pairs(left_val, right_val):
    return (left_val[0] + right_val[0], left_val[1] + right_val[1])

def direction_model(first_gain, sky_model, second_gain):
    first_mat = split_entries(first_gain)
    sky_mat = split_entries(sky_model)
    second_mat = split_entries(second_gain)
    product = [[add_pairs(times_pair(first_mat[left_index][0], sky_mat[0][right_index]), times_pair(first_mat[left_index][1], sky_mat[1][right_index])) for right_index in range(2)] for left_index in range(2)]
    result = [[add_pairs(times_conj(product[left_index][0], second_mat[right_index][0]), times_conj(product[left_index][1], second_mat[right_index][1])) for right_index in range(2)] for left_index in range(2)]
    components = []
    for left_index in range(2):
        for right_index in range(2):
            components.append(result[left_index][right_index][0])
            components.append(result[left_index][right_index][1])
    return jnp.stack(components, axis=0)

def model_sum(gain_block, first_station, second_station, sky_model):
    first_gain = jnp.take(gain_block, first_station, axis=2)
    second_gain = jnp.take(gain_block, second_station, axis=2)
    return lax.optimization_barrier(jnp.sum(direction_model(first_gain, sky_model, second_gain), axis=1))

def gradient_all(jones, visibilities, coherency, stations):
    gain_blocks = jones.reshape(NCH, 8, K, S)
    weight = np.sqrt(S / (2.0 * TIMES * BL_DEV)).astype(np.float32)

    def per_time(running, inputs):
        vis_slot, coh_slot, pair_slot = inputs

        def per_channel(gain_block, vis_chan, coh_chan):
            model_vis, pullback = jax.vjp(lambda gains: model_sum(gains, pair_slot[0], pair_slot[1], coh_chan.astype(jnp.float32)), gain_block)
            return pullback(-weight * (vis_chan - model_vis))[0]
        return (running + jax.vmap(per_channel)(gain_blocks, vis_slot, coh_slot), None)
    running, _ = lax.scan(per_time, jnp.zeros((NCH, 8, K, S), jnp.float32), (visibilities, coherency, stations))
    return running.reshape(NCH, 8, K * S)

def reference(visibilities, coherency, stations, jones, dual, cluster, rho_table):
    rho_dir = lax.optimization_barrier(jnp.sum(jnp.where(cluster[:, None] == jnp.arange(NCL, dtype=jnp.int32)[None, :], rho_table[None, :], jnp.float32(0.0)), axis=1))
    rho_flat = jnp.repeat(rho_dir, S)
    poly_table = jnp.asarray(poly_basis(NCH, NP))

    def consensus_of(state, dual_now):
        return jnp.einsum('fj,fcn->jcn', poly_table, state + dual_now / rho_flat, precision=highest)

    def project(poly_coef):
        return jnp.einsum('fj,jcn->fcn', poly_table, poly_coef, precision=highest)
    poly_coef = consensus_of(jones, dual)
    fitted = project(poly_coef)
    for iteration in range(ITERS):
        gradient = gradient_all(jones, visibilities, coherency, stations)
        descent = gradient + dual + rho_flat * (jones - fitted)
        scale = jnp.sqrt(lax.optimization_barrier(jnp.mean(descent * descent, axis=(1, 2), keepdims=True)) + epsilon)
        jones = jones - step_size * descent / scale
        poly_coef = consensus_of(jones, dual)
        fitted = project(poly_coef)
        dual = dual + rho_flat * (jones - fitted)
    return (jones, dual, poly_coef)
```

```python
import functools
import math

import jax
import jax.numpy as jnp
import numpy as np
from jax import lax
from jax.experimental import pallas as pl
from jax.experimental.pallas import tpu as pltpu
from jax.sharding import PartitionSpec as P

ITERS = 2
MESH = pl.DeviceIdType.MESH
ROWS = 8

step_size = 0.5
epsilon = 1e-06


def poly_basis(channels, degrees):
    points = np.linspace(-1.0, 1.0, channels)
    columns = []
    for degree in range(degrees):
        column = points**degree
        for earlier in columns:
            column = column - np.dot(earlier, column) * earlier
        column = column / np.sqrt(np.dot(column, column))
        columns.append(column)
    return np.stack(columns, axis=1).astype(np.float32)


def split_entries(parts):
    return [[(parts[4 * i + 2 * j], parts[4 * i + 2 * j + 1]) for j in range(2)] for i in range(2)]


def join_entries(mat):
    return [part for row in mat for entry in row for part in entry]


def times_pair(a, b):
    return (a[0] * b[0] - a[1] * b[1], a[0] * b[1] + a[1] * b[0])


def times_conj(a, b):
    return (a[0] * b[0] + a[1] * b[1], a[1] * b[0] - a[0] * b[1])


def add_pairs(a, b):
    return (a[0] + b[0], a[1] + b[1])


def mat_mul(a, b):
    return [[add_pairs(times_pair(a[i][0], b[0][j]), times_pair(a[i][1], b[1][j])) for j in range(2)] for i in range(2)]


def mat_mul_right_h(a, b):
    return [[add_pairs(times_conj(a[i][0], b[j][0]), times_conj(a[i][1], b[j][1])) for j in range(2)] for i in range(2)]


def mat_mul_left_h(a, b):
    return [[add_pairs(times_conj(b[0][j], a[0][i]), times_conj(b[1][j], a[1][i])) for j in range(2)] for i in range(2)]


def kernel(
    T, F, nd, S, K, N, basis, weight,
    vis_ref, coh_ref, st_ref, jones_ref, dual_ref, cluster_ref, table_ref,
    jones_out, dual_out, poly_out,
    coh_in, coh32, st_all, oh, tab, gp, abuf, xbuf, partial, part_in, res, acc, jn, du, de, fit, rho, sq,
    st_ss, st_rs, coh_ss, coh_rs, pa_ss, pa_rs, re_ss, re_rs, in_ss, in_rs, de_ss, de_rs, sq_ss, sq_rs,
):
    me = lax.axis_index("tm")
    fi = lax.axis_index("freq")
    g = ROWS // nd
    groups = T // g
    L = nd * S
    degrees = basis.shape[1]
    own_group = me // g

    def st_copy(src, to):
        return pltpu.make_async_remote_copy(
            src_ref=st_all.at[src], dst_ref=st_all.at[src], send_sem=st_ss.at[to], recv_sem=st_rs.at[src],
            device_id={"tm": to}, device_id_type=MESH)

    def coh_copy(src, to):
        return pltpu.make_async_remote_copy(
            src_ref=coh_ref.at[to], dst_ref=coh_in.at[src], send_sem=coh_ss.at[to], recv_sem=coh_rs.at[src],
            device_id={"tm": to}, device_id_type=MESH)

    def part_copy(it, src, to):
        return pltpu.make_async_remote_copy(
            src_ref=partial.at[it, to], dst_ref=part_in.at[it, src], send_sem=pa_ss.at[it, to],
            recv_sem=pa_rs.at[it, src], device_id={"tm": to}, device_id_type=MESH)

    def res_copy(it, src, to):
        return pltpu.make_async_remote_copy(
            src_ref=res.at[it, src], dst_ref=res.at[it, src], send_sem=re_ss.at[it, to],
            recv_sem=re_rs.at[it, src], device_id={"tm": to}, device_id_type=MESH)

    def state_copy(which, src, to):
        ref = (jn, du)[which]
        return pltpu.make_async_remote_copy(
            src_ref=ref.at[src], dst_ref=ref.at[src], send_sem=in_ss.at[which, to], recv_sem=in_rs.at[which, src],
            device_id={"freq": to}, device_id_type=MESH)

    def de_copy(it, src, to):
        return pltpu.make_async_remote_copy(
            src_ref=de.at[it, src], dst_ref=de.at[it, src], send_sem=de_ss.at[it, to], recv_sem=de_rs.at[it, src],
            device_id={"freq": to}, device_id_type=MESH)

    def sq_copy(it, to_f, to_t):
        mine = fi * T + me
        return pltpu.make_async_remote_copy(
            src_ref=sq.at[it, mine], dst_ref=sq.at[it, mine], send_sem=sq_ss.at[it], recv_sem=sq_rs.at[it],
            device_id={"tm": to_t, "freq": to_f}, device_id_type=MESH)

    def sq_all(it):
        span = sq.at[it, pl.ds(0, F * T - 1)]
        return pltpu.make_async_remote_copy(
            src_ref=span, dst_ref=span, send_sem=sq_ss.at[it], recv_sem=sq_rs.at[it],
            device_id={"tm": me, "freq": fi}, device_id_type=MESH)

    def each_peer(fn):
        def one(o, _):
            fn(lax.rem(me + o, T))
            return 0
        lax.fori_loop(1, T, one, 0)

    def each_other(fn):
        def one(o, _):
            fn(lax.rem(fi * T + me + o, F * T))
            return 0
        lax.fori_loop(1, F * T, one, 0)

    st_all[me] = st_ref[...]
    jn[fi] = jones_ref[...]
    du[fi] = dual_ref[...]
    barrier = pltpu.get_barrier_semaphore()

    def greet(d):
        pl.semaphore_signal(barrier, inc=1, device_id={"tm": lax.rem(d, T), "freq": d // T}, device_id_type=MESH)

    each_other(greet)
    pl.semaphore_wait(barrier, F * T - 1)

    each_peer(lambda j: st_copy(me, j).start())
    each_peer(lambda j: coh_copy(me, j).start())
    for o in range(1, F):
        to = lax.rem(fi + o, F)
        state_copy(0, fi, to).start()
        state_copy(1, fi, to).start()
    coh_in[me] = coh_ref[me]

    for d in range(nd):
        value = table_ref[cluster_ref[me * nd + d]]
        rho[:, d * S:(d + 1) * S] = jnp.full((ROWS, S), value, jnp.float32)

    slot_n = lax.broadcasted_iota(jnp.int32, (ROWS, N), 0) // nd
    slot_c = lax.broadcasted_iota(jnp.int32, (ROWS, 128), 0) // nd

    def set_table():
        now = jn[fi]
        for d in range(nd):
            piece = now[:, d * S:(d + 1) * S]
            high = piece.astype(jnp.bfloat16).astype(jnp.float32)
            low = piece - high
            for s in range(g):
                for q in range(S // 128):
                    part = high if s % 2 == 0 else low
                    tab[q, pl.ds(s * nd + d, 8, stride=8), :] = part[:, q * 128:(q + 1) * 128]

    def gather_group(it, p):
        packed = [None, None]
        table = jnp.concatenate([tab[q] for q in range(S // 128)], axis=1).astype(jnp.bfloat16)
        for tt in range(g):
            t = p * g + tt
            if it == 0:
                @pl.when(t != me)
                def _():
                    st_copy(t, me).wait_recv()
                for e in range(2):
                    row = st_all[t, e:e + 1, :]
                    for lo in range(0, S, 64):
                        ids = lax.broadcasted_iota(jnp.int32, (64, N), 0) + lo
                        oh[t, e, lo:lo + 64, :] = jnp.where(ids == row, 1.0, 0.0).astype(jnp.bfloat16)
            for e in range(2):
                got = jnp.dot(table, oh[t, e], preferred_element_type=jnp.float32)
                tiles = []
                for c in range(8):
                    tile = got[8 * c:8 * c + 8, :]
                    tile = tile + pltpu.roll(tile, nd, 0)
                    tiles.append(tile if tt == 0 else jnp.where(slot_n == tt, tile, packed[e][c]))
                packed[e] = tiles
        for e in range(2):
            for c in range(8):
                gp[p, e, c] = packed[e][c]

    def forward_group(it, p):
        if it == 0:
            tiles = []
            for tt in range(g):
                t = p * g + tt

                @pl.when(t != me)
                def _():
                    coh_copy(t, me).wait_recv()
                tiles.append(coh_in[t].astype(jnp.float32))
            for c in range(8):
                out = None
                for tt in range(g):
                    tile = tiles[tt][8 * (c // g):8 * (c // g) + 8, :]
                    shift = ((tt - c % g) % g) * nd
                    if shift:
                        tile = pltpu.roll(tile, shift, 0)
                    out = tile if tt == 0 else jnp.where(slot_n == tt, tile, out)
                coh32[p, c] = out
        for lo in range(0, N, 128):
            lanes = slice(lo, lo + 128)
            first = split_entries([gp[p, 0, c, :, lanes] for c in range(8)])
            second = split_entries([gp[p, 1, c, :, lanes] for c in range(8)])
            sky = split_entries([coh32[p, c, :, lanes] for c in range(8)])
            prod = mat_mul(first, sky)
            for c, part in enumerate(join_entries(prod)):
                abuf[p, c, :, lanes] = part
            model = join_entries(mat_mul_right_h(prod, second))
            for c in range(8):
                total = model[c]
                width = 1
                while width < nd:
                    total = total + pltpu.roll(total, ROWS - width, 0)
                    width *= 2
                for tt in range(g):
                    partial[it, p * g + tt, c:c + 1, lanes] = total[tt * nd:tt * nd + 1, :]
        for tt in range(g):
            t = p * g + tt

            @pl.when(t != me)
            def _():
                part_copy(it, me, t).start()

    def backward_group(it, p):
        for tt in range(g):
            t = p * g + tt

            @pl.when(t != me)
            def _():
                res_copy(it, t, me).wait_recv()
        for lo in range(0, N, 128):
            lanes = slice(lo, lo + 128)
            prod = split_entries([abuf[p, c, :, lanes] for c in range(8)])
            second = split_entries([gp[p, 1, c, :, lanes] for c in range(8)])
            sky = split_entries([coh32[p, c, :, lanes] for c in range(8)])
            resid = []
            for c in range(8):
                out = None
                for tt in range(g):
                    row = jnp.broadcast_to(res[it, p * g + tt, c:c + 1, lanes], (ROWS, 128))
                    out = row if tt == 0 else jnp.where(slot_c == tt, row, out)
                resid.append(out)
            resid = split_entries(resid)
            grads = (
                join_entries(mat_mul(resid, mat_mul_right_h(second, sky))),
                join_entries(mat_mul_left_h(resid, prod)),
            )
            for e in range(2):
                highs = [x.astype(jnp.bfloat16).astype(jnp.float32) for x in grads[e]]
                lows = [pltpu.roll(x - h, nd, 0) for x, h in zip(grads[e], highs)]
                for tt in range(g):
                    outs = []
                    for h, l in zip(highs, lows):
                        rest = l if g == 2 else jnp.where(slot_c == (tt + 1) % g, l, 0.0)
                        outs.append(jnp.where(slot_c == tt, h, rest))
                    xbuf[e, tt, :, lanes] = jnp.concatenate(outs, axis=0).astype(jnp.bfloat16)
        total = jnp.concatenate([acc[q] for q in range(S // 128)], axis=1)
        for tt in range(g):
            for e in range(2):
                total = total + lax.dot_general(
                    xbuf[e, tt], oh[p * g + tt, e], (((1,), (1,)), ((), ())), preferred_element_type=jnp.float32)
        for q in range(S // 128):
            acc[q] = total[:, q * 128:(q + 1) * 128]

    def consensus():
        sums = [jn[f] + du[f] / rho[...] for f in range(F)]
        for j in range(degrees):
            total = None
            for f in range(F):
                term = float(basis[f, j]) * sums[f]
                total = term if total is None else total + term
            poly_out[j] = total
        for f in range(F):
            total = None
            for j in range(degrees):
                term = float(basis[f, j]) * poly_out[j]
                total = term if total is None else total + term
            fit[f] = total

    set_table()

    for it in range(ITERS):
        def gather_step(i, _):
            gather_group(it, lax.rem(own_group - 1 - i + 2 * groups, groups))
            return 0

        def forward_step(i, _):
            forward_group(it, lax.rem(own_group - 1 - i + 2 * groups, groups))
            return 0

        def backward_step(i, _):
            backward_group(it, lax.rem(own_group - 1 - i + 2 * groups, groups))
            return 0

        lax.fori_loop(0, groups, gather_step, 0)
        lax.fori_loop(0, groups, forward_step, 0)
        if it == 0:
            for o in range(1, F):
                other = lax.rem(fi + o, F)
                state_copy(0, other, fi).wait_recv()
                state_copy(1, other, fi).wait_recv()
            consensus()

        def add_part(o, total):
            src = lax.rem(me - o + T, T)
            part_copy(it, src, me).wait_recv()
            return total + part_in[it, src]

        model = lax.fori_loop(1, T, add_part, partial[it, me])
        res[it, me] = weight * (model - vis_ref[...])
        each_peer(lambda j: res_copy(it, me, j).start())
        acc[...] = jnp.zeros_like(acc)
        lax.fori_loop(0, groups, backward_step, 0)

        for d in range(nd):
            for q in range(S // 128):
                total = None
                for s in range(g):
                    term = acc[q, pl.ds(s * nd + d, 8, stride=8), :]
                    total = term if total is None else total + term
                de[it, fi, :, d * S + q * 128:d * S + (q + 1) * 128] = total
        descent = de[it, fi] + du[fi] + rho[...] * (jn[fi] - fit[fi])
        de[it, fi] = descent
        squares = descent * descent
        total = squares[:, 0:128]
        for lo in range(128, L, 128):
            total = total + squares[:, lo:lo + 128]
        sq[it, fi * T + me] = total
        each_other(lambda d: sq_copy(it, d // T, lax.rem(d, T)).start())
        for o in range(1, F):
            de_copy(it, fi, lax.rem(fi + o, F)).start()
        sq_all(it).wait_recv()
        for o in range(1, F):
            de_copy(it, lax.rem(fi + o, F), fi).wait_recv()
        if it == 0:
            for o in range(1, F):
                other = lax.rem(fi + o, F)
                state_copy(0, fi, other).wait_send()
                state_copy(1, fi, other).wait_send()
        for f in range(F):
            tile = jnp.sum(sq[it, pl.ds(f * T, T)], axis=0)
            whole = jnp.sum(jnp.sum(tile, axis=1, keepdims=True), axis=0, keepdims=True)
            scale = jnp.sqrt(whole / (8.0 * K * S) + epsilon)
            jn[f] = jn[f] - step_size * de[it, f] / scale
        if it + 1 < ITERS:
            set_table()
        consensus()
        for f in range(F):
            du[f] = du[f] + rho[...] * (jn[f] - fit[f])

    jones_out[...] = jn[fi]
    dual_out[...] = du[fi]

    def drain(j):
        st_copy(me, j).wait_send()
        coh_copy(me, j).wait_send()
        for it in range(ITERS):
            part_copy(it, me, j).wait_send()
            res_copy(it, me, j).wait_send()

    each_peer(drain)
    for it in range(ITERS):
        sq_all(it).wait_send()
        for o in range(1, F):
            de_copy(it, fi, lax.rem(fi + o, F)).wait_send()


def body(visibilities, coherency, stations, jones, dual, cluster, rho_table):
    T = lax.axis_size("tm")
    F = lax.axis_size("freq")
    K, N = coherency.shape[3], coherency.shape[4]
    L = jones.shape[2]
    nd = K // T
    S = L // nd
    g = ROWS // nd
    basis = poly_basis(F, min(3, F - 1))
    degrees = basis.shape[1]
    weight = np.float32(math.sqrt(S / (2.0 * T * N)))
    blocks = coherency[0, 0].reshape(8, T, nd, N).transpose(1, 0, 2, 3).reshape(T, 8 * nd, N)
    vmem = pl.BlockSpec(memory_space=pltpu.VMEM)
    smem = pl.BlockSpec(memory_space=pltpu.SMEM)
    f32, bf16 = jnp.float32, jnp.bfloat16
    dma = pltpu.SemaphoreType.DMA
    jones_out, dual_out, poly = pl.pallas_call(
        functools.partial(kernel, T, F, nd, S, K, N, basis, weight),
        out_shape=(
            jax.ShapeDtypeStruct((8, L), f32),
            jax.ShapeDtypeStruct((8, L), f32),
            jax.ShapeDtypeStruct((degrees, 8, L), f32),
        ),
        in_specs=[vmem] * 5 + [smem] * 2,
        out_specs=(vmem, vmem, vmem),
        scratch_shapes=[
            pltpu.VMEM((T, 8 * nd, N), bf16),
            pltpu.VMEM((T // g, 8, 8, N), f32),
            pltpu.VMEM((T, 2, N), jnp.int32),
            pltpu.VMEM((T, 2, S, N), bf16),
            pltpu.VMEM((S // 128, 64, 128), f32),
            pltpu.VMEM((T // g, 2, 8, 8, N), f32),
            pltpu.VMEM((T // g, 8, 8, N), f32),
            pltpu.VMEM((2, g, 64, N), bf16),
            pltpu.VMEM((ITERS, T, 8, N), f32),
            pltpu.VMEM((ITERS, T, 8, N), f32),
            pltpu.VMEM((ITERS, T, 8, N), f32),
            pltpu.VMEM((S // 128, 64, 128), f32),
            pltpu.VMEM((F, 8, L), f32),
            pltpu.VMEM((F, 8, L), f32),
            pltpu.VMEM((ITERS, F, 8, L), f32),
            pltpu.VMEM((F, 8, L), f32),
            pltpu.VMEM((8, L), f32),
            pltpu.VMEM((ITERS, F * T, 8, 128), f32),
            dma((T,)), dma((T,)), dma((T,)), dma((T,)),
            dma((ITERS, T)), dma((ITERS, T)), dma((ITERS, T)), dma((ITERS, T)),
            dma((2, F)), dma((2, F)), dma((ITERS, F)), dma((ITERS, F)), dma((ITERS,)), dma((ITERS,)),
        ],
        compiler_params=pltpu.CompilerParams(
            collective_id=0, has_side_effects=True, vmem_limit_bytes=56 * 1024 * 1024),
        cost_estimate=pl.CostEstimate(flops=10**10, bytes_accessed=10**7, transcendentals=0),
    )(visibilities[0, 0], blocks, stations[0], jones[0], dual[0], cluster, rho_table)
    return jones_out[None], dual_out[None], poly


def solution(mesh):
    return jax.shard_map(
        body,
        mesh=mesh,
        in_specs=(
            P("tm", "freq", None, None),
            P("tm", "freq", None, None, None),
            P("tm", None, None),
            P("freq", None, "tm"),
            P("freq", None, "tm"),
            P(),
            P(),
        ),
        out_specs=(P("freq", None, "tm"), P("freq", None, "tm"), P(None, None, "tm")),
        check_vma=False,
    )
```

```python
import functools
import math

import jax
import jax.numpy as jnp
import numpy as np
from jax import lax
from jax.experimental import pallas as pl
from jax.experimental.pallas import tpu as pltpu
from jax.sharding import PartitionSpec as P

ITERS = 2
MESH = pl.DeviceIdType.MESH
ROWS = 8

step_size = 0.5
epsilon = 1e-06


def poly_basis(channels, degrees):
    points = np.linspace(-1.0, 1.0, channels)
    columns = []
    for degree in range(degrees):
        column = points**degree
        for earlier in columns:
            column = column - np.dot(earlier, column) * earlier
        column = column / np.sqrt(np.dot(column, column))
        columns.append(column)
    return np.stack(columns, axis=1).astype(np.float32)


def split_entries(parts):
    return [[(parts[4 * i + 2 * j], parts[4 * i + 2 * j + 1]) for j in range(2)] for i in range(2)]


def join_entries(mat):
    return [part for row in mat for entry in row for part in entry]


def times_pair(a, b):
    return (a[0] * b[0] - a[1] * b[1], a[0] * b[1] + a[1] * b[0])


def times_conj(a, b):
    return (a[0] * b[0] + a[1] * b[1], a[1] * b[0] - a[0] * b[1])


def add_pairs(a, b):
    return (a[0] + b[0], a[1] + b[1])


def mat_mul(a, b):
    return [[add_pairs(times_pair(a[i][0], b[0][j]), times_pair(a[i][1], b[1][j])) for j in range(2)] for i in range(2)]


def mat_mul_right_h(a, b):
    return [[add_pairs(times_conj(a[i][0], b[j][0]), times_conj(a[i][1], b[j][1])) for j in range(2)] for i in range(2)]


def mat_mul_left_h(a, b):
    return [[add_pairs(times_conj(b[0][j], a[0][i]), times_conj(b[1][j], a[1][i])) for j in range(2)] for i in range(2)]


def kernel(
    T, F, Z, nd, S, K, N, basis, weight,
    vis_ref, coh_hbm, st_ref, jones_ref, dual_ref, cluster_ref, table_ref,
    jones_out, dual_out, poly_out,
    coh_raw, coh_out, coh_in, st_all, oh, tab, tabs, gz, zde, gp, abuf, xbuf, partial, part_in, res, acc, gout, gin,
    jn, du, de, fit, rho, sq,
    raw_sem, st_ss, st_rs, coh_ss, coh_rs, gz_ss, gz_rs, zd_ss, zd_rs, pa_ss, pa_rs, re_ss, re_rs, go_ss, go_rs,
    in_ss, in_rs, de_ss, de_rs, sq_ss, sq_rs,
):
    me = lax.axis_index("tm")
    fi = lax.axis_index("freq")
    Q = T // Z
    z, q = me // Q, lax.rem(me, Q)
    D = Z * nd
    tiles = D // ROWS
    g = ROWS // nd
    L = nd * S
    lane_tiles = S // 128
    degrees = basis.shape[1]

    def remote(src, dst, send, recv, to):
        return pltpu.make_async_remote_copy(
            src_ref=src, dst_ref=dst, send_sem=send, recv_sem=recv, device_id=to, device_id_type=MESH)

    def plane(u):
        return {"tm": z * Q + u}

    def column(v):
        return {"tm": v * Q + q}

    def st_copy(src, to):
        return remote(st_all.at[src], st_all.at[src], st_ss.at[to], st_rs.at[src], plane(to))

    def coh_copy(src, to):
        return remote(coh_out.at[to], coh_in.at[src], coh_ss.at[to], coh_rs.at[src], plane(to))

    def part_copy(it, src, to):
        return remote(partial.at[it, to], part_in.at[it, src], pa_ss.at[it, to], pa_rs.at[it, src], plane(to))

    def res_copy(it, src, to):
        return remote(res.at[it, src], res.at[it, src], re_ss.at[it, to], re_rs.at[it, src], plane(to))

    def gz_copy(src, to):
        return remote(gz.at[src], gz.at[src], gz_ss.at[to], gz_rs.at[src], column(to))

    def zd_copy(it, src, to):
        return remote(de.at[it, fi], zde.at[it, src], zd_ss.at[it, to], zd_rs.at[it, src], column(to))

    def go_copy(it, src, to):
        return remote(gout.at[it, to], gin.at[it, src], go_ss.at[it, to], go_rs.at[it, src], column(to))

    def state_copy(which, src, to):
        ref = (jn, du)[which]
        return remote(ref.at[src], ref.at[src], in_ss.at[which, to], in_rs.at[which, src], {"freq": to})

    def de_copy(it, src, to):
        return remote(de.at[it, src], de.at[it, src], de_ss.at[it, to], de_rs.at[it, src], {"freq": to})

    def sq_copy(it, to_f, to_t):
        mine = fi * T + me
        return remote(sq.at[it, mine], sq.at[it, mine], sq_ss.at[it], sq_rs.at[it], {"tm": to_t, "freq": to_f})

    def sq_all(it):
        span = sq.at[it, pl.ds(0, F * T - 1)]
        return remote(span, span, sq_ss.at[it], sq_rs.at[it], {"tm": me, "freq": fi})

    def each_other(fn):
        def one(o, _):
            fn(lax.rem(fi * T + me + o, F * T))
            return 0
        lax.fori_loop(1, F * T, one, 0)

    plane_next = [lax.rem(q + o, Q) for o in range(1, Q)]
    plane_from = [lax.rem(q - o + Q, Q) for o in range(1, Q)]
    column_others = [lax.rem(z + o, Z) for o in range(1, Z)]
    freq_others = [lax.rem(fi + o, F) for o in range(1, F)]

    raw = pltpu.make_async_copy(coh_hbm, coh_raw, raw_sem)
    raw.start()
    barrier = pltpu.get_barrier_semaphore()

    def greet(d):
        pl.semaphore_signal(barrier, inc=1, device_id={"tm": lax.rem(d, T), "freq": d // T}, device_id_type=MESH)

    each_other(greet)
    st_all[q] = st_ref[...]
    gz[z] = jones_ref[...]
    jn[fi] = jones_ref[...]
    du[fi] = dual_ref[...]
    for d in range(nd):
        value = table_ref[cluster_ref[me * nd + d]]
        rho[:, d * S:(d + 1) * S] = jnp.full((ROWS, S), value, jnp.float32)
    pl.semaphore_wait(barrier, F * T - 1)

    for to in plane_next:
        st_copy(q, to).start()
    for to in column_others:
        gz_copy(z, to).start()
    raw.wait()

    slot = lax.broadcasted_iota(jnp.int32, (ROWS, N), 0) // nd
    for c in range(8):
        full = coh_raw[c].astype(jnp.float32)
        for u in range(Q):
            rows = []
            for m in range(tiles):
                out = None
                for s in range(g):
                    unit = (m * g + s) * Q + u
                    tile = full[8 * (unit // g):8 * (unit // g) + 8, :]
                    shift = ((s - unit % g) % g) * nd
                    if shift:
                        tile = pltpu.roll(tile, shift, 0)
                    out = tile if s == 0 else jnp.where(slot == s, tile, out)
                rows.append(out)
            block = rows[0] if tiles == 1 else jnp.concatenate(rows, axis=0)
            coh_out[u, c * D:(c + 1) * D, :] = block.astype(jnp.bfloat16)
    for to in plane_next:
        coh_copy(q, to).start()
    coh_in[q] = coh_out[q]
    for to in freq_others:
        state_copy(0, fi, to).start()
        state_copy(1, fi, to).start()

    def build(i, _):
        u = lax.rem(q - i + Q, Q)

        @pl.when(u != q)
        def _():
            st_copy(u, q).wait_recv()
        for e in range(2):
            row = st_all[u, e:e + 1, :]
            for lo in range(0, S, 64):
                ids = lax.broadcasted_iota(jnp.int32, (64, N), 0) + lo
                oh[u, e, lo:lo + 64, :] = jnp.where(ids == row, 1.0, 0.0).astype(jnp.bfloat16)
        return 0

    lax.fori_loop(0, Q, build, 0)

    def set_table():
        for v in range(Z):
            now = gz[v]
            for d in range(nd):
                piece = now[:, d * S:(d + 1) * S]
                high = piece.astype(jnp.bfloat16).astype(jnp.float32)
                low = piece - high
                for k in range(lane_tiles):
                    lanes = slice(k * 128, (k + 1) * 128)
                    tabs[0, k, pl.ds(v * nd + d, 8, stride=D), :] = high[:, lanes]
                    tabs[1, k, pl.ds(v * nd + d, 8, stride=D), :] = low[:, lanes]
        for h in range(2):
            for k in range(lane_tiles):
                tab[h, :, k * 128:(k + 1) * 128] = tabs[h, k].astype(jnp.bfloat16)

    def gather_time(u):
        for e in range(2):
            gp[u, e] = (
                jnp.dot(tab[0], oh[u, e], preferred_element_type=jnp.float32)
                + jnp.dot(tab[1], oh[u, e], preferred_element_type=jnp.float32))

    def tile_rows(c, m):
        return slice(c * D + m * ROWS, c * D + (m + 1) * ROWS)

    def sky_tiles(u, lanes):
        sky = [coh_in[u, c * D:(c + 1) * D, lanes].astype(jnp.float32) for c in range(8)]
        return [split_entries([part[m * ROWS:(m + 1) * ROWS] for part in sky]) for m in range(tiles)]

    def forward_time(it, u):
        for lo in range(0, N, 128):
            lanes = slice(lo, lo + 128)
            sky = sky_tiles(u, lanes)
            sums = None
            for m in range(tiles):
                first = split_entries([gp[u, 0, tile_rows(c, m), lanes] for c in range(8)])
                second = split_entries([gp[u, 1, tile_rows(c, m), lanes] for c in range(8)])
                prod = mat_mul(first, sky[m])
                for c, part in enumerate(join_entries(prod)):
                    abuf[u, tile_rows(c, m), lanes] = part
                model = join_entries(mat_mul_right_h(prod, second))
                sums = model if sums is None else [x + y for x, y in zip(sums, model)]
            for c in range(8):
                partial[it, u, c:c + 1, lanes] = jnp.sum(sums[c], axis=0, keepdims=True)

        @pl.when(u != q)
        def _():
            part_copy(it, q, u).start()

    def backward_time(it, u):
        @pl.when(u != q)
        def _():
            res_copy(it, u, q).wait_recv()
        for lo in range(0, N, 128):
            lanes = slice(lo, lo + 128)
            sky = sky_tiles(u, lanes)
            resid = split_entries([
                jnp.broadcast_to(res[it, u, c:c + 1, lanes], (ROWS, 128)) for c in range(8)])
            grads = [[None] * (8 * tiles), [None] * (8 * tiles)]
            for m in range(tiles):
                prod = split_entries([abuf[u, tile_rows(c, m), lanes] for c in range(8)])
                second = split_entries([gp[u, 1, tile_rows(c, m), lanes] for c in range(8)])
                first_grad = join_entries(mat_mul(resid, mat_mul_right_h(second, sky[m])))
                second_grad = join_entries(mat_mul_left_h(resid, prod))
                for c in range(8):
                    grads[0][c * tiles + m] = first_grad[c]
                    grads[1][c * tiles + m] = second_grad[c]
            for e in range(2):
                for pair in range(4 * tiles):
                    both = jnp.concatenate(grads[e][2 * pair:2 * pair + 2], axis=0)
                    high = both.astype(jnp.bfloat16)
                    low = (both - high.astype(jnp.float32)).astype(jnp.bfloat16)
                    xbuf[0, e, 16 * pair:16 * pair + 16, lanes] = high
                    xbuf[1, e, 16 * pair:16 * pair + 16, lanes] = low
        for k in range(lane_tiles):
            total = acc[k]
            for e in range(2):
                for h in range(2):
                    total = total + lax.dot_general(
                        xbuf[h, e], oh[u, e, k * 128:(k + 1) * 128, :], (((1,), (1,)), ((), ())),
                        preferred_element_type=jnp.float32)
            acc[k] = total

    def consensus():
        sums = [jn[f] + du[f] / rho[...] for f in range(F)]
        for j in range(degrees):
            total = None
            for f in range(F):
                term = float(basis[f, j]) * sums[f]
                total = term if total is None else total + term
            poly_out[j] = total
        for f in range(F):
            total = None
            for j in range(degrees):
                term = float(basis[f, j]) * poly_out[j]
                total = term if total is None else total + term
            fit[f] = total

    for v in column_others:
        gz_copy(v, z).wait_recv()

    for it in range(ITERS):
        set_table()
        if it == 0:
            def gather_step(i, _):
                gather_time(lax.rem(q - i + Q, Q))
                return 0

            def forward_step(i, _):
                u = lax.rem(q - i + Q, Q)

                @pl.when(u != q)
                def _():
                    coh_copy(u, q).wait_recv()
                forward_time(it, u)
                return 0

            lax.fori_loop(0, Q, gather_step, 0)
            lax.fori_loop(0, Q, forward_step, 0)
            for f in freq_others:
                state_copy(0, f, fi).wait_recv()
                state_copy(1, f, fi).wait_recv()
            consensus()
        else:
            def both_step(i, _):
                u = lax.rem(q + 1 + i, Q)
                gather_time(u)
                forward_time(it, u)
                return 0

            lax.fori_loop(0, Q, both_step, 0)

        model = partial[it, q]
        for u in plane_from:
            part_copy(it, u, q).wait_recv()
            model = model + part_in[it, u]
        res[it, q] = weight * (model - vis_ref[...])
        for to in plane_next:
            res_copy(it, q, to).start()
        acc[...] = jnp.zeros_like(acc)

        def backward_step(i, _):
            backward_time(it, lax.rem(q - i + Q, Q))
            return 0

        lax.fori_loop(0, Q, backward_step, 0)

        for v in range(Z):
            for d in range(nd):
                for k in range(lane_tiles):
                    gout[it, v, :, d * S + k * 128:d * S + (k + 1) * 128] = acc[k, pl.ds(v * nd + d, 8, stride=D), :]
        for v in column_others:
            go_copy(it, z, v).start()
        grad = gout[it, z]
        for v in column_others:
            go_copy(it, v, z).wait_recv()
            grad = grad + gin[it, v]
        descent = grad + du[fi] + rho[...] * (jn[fi] - fit[fi])
        de[it, fi] = descent
        squares = descent * descent
        total = squares[:, 0:128]
        for lo in range(128, L, 128):
            total = total + squares[:, lo:lo + 128]
        sq[it, fi * T + me] = total
        each_other(lambda d: sq_copy(it, d // T, lax.rem(d, T)).start())
        last = it + 1 == ITERS
        if not last:
            for v in column_others:
                zd_copy(it, z, v).start()
        for f in freq_others:
            de_copy(it, fi, f).start()
        sq_all(it).wait_recv()
        for f in freq_others:
            de_copy(it, f, fi).wait_recv()
        if it == 0:
            for f in freq_others:
                state_copy(0, fi, f).wait_send()
                state_copy(1, fi, f).wait_send()
            for v in column_others:
                gz_copy(z, v).wait_send()
        scales = []
        for f in range(F):
            tile = jnp.sum(sq[it, pl.ds(f * T, T)], axis=0)
            whole = jnp.sum(jnp.sum(tile, axis=1, keepdims=True), axis=0, keepdims=True)
            scale = jnp.sqrt(whole / (8.0 * K * S) + epsilon)
            scales.append(scale)
            jn[f] = jn[f] - step_size * de[it, f] / scale
        consensus()
        for f in range(F):
            du[f] = du[f] + rho[...] * (jn[f] - fit[f])
        if not last:
            own = scales[0]
            for f in range(1, F):
                own = jnp.where(fi == f, scales[f], own)
            gz[z] = jn[fi]
            for v in column_others:
                zd_copy(it, v, z).wait_recv()
                gz[v] = gz[v] - step_size * zde[it, v] / own

    jones_out[...] = jn[fi]
    dual_out[...] = du[fi]
    for to in plane_next:
        st_copy(q, to).wait_send()
        coh_copy(q, to).wait_send()
        for it in range(ITERS):
            part_copy(it, q, to).wait_send()
            res_copy(it, q, to).wait_send()
    for it in range(ITERS):
        for v in column_others:
            go_copy(it, z, v).wait_send()
            if it + 1 < ITERS:
                zd_copy(it, z, v).wait_send()
        sq_all(it).wait_send()
        for f in freq_others:
            de_copy(it, fi, f).wait_send()


def body(visibilities, coherency, stations, jones, dual, cluster, rho_table):
    T = lax.axis_size("tm")
    F = lax.axis_size("freq")
    K, N = coherency.shape[3], coherency.shape[4]
    L = jones.shape[2]
    nd = K // T
    S = L // nd
    Z = math.gcd(T, 4)
    Q = T // Z
    D = Z * nd
    basis = poly_basis(F, min(3, F - 1))
    degrees = basis.shape[1]
    weight = np.float32(math.sqrt(S / (2.0 * T * N)))
    vmem = pl.BlockSpec(memory_space=pltpu.VMEM)
    smem = pl.BlockSpec(memory_space=pltpu.SMEM)
    anywhere = pl.BlockSpec(memory_space=pl.ANY)
    f32, bf16 = jnp.float32, jnp.bfloat16
    dma = pltpu.SemaphoreType.DMA
    jones_out, dual_out, poly = pl.pallas_call(
        functools.partial(kernel, T, F, Z, nd, S, K, N, basis, weight),
        out_shape=(
            jax.ShapeDtypeStruct((8, L), f32),
            jax.ShapeDtypeStruct((8, L), f32),
            jax.ShapeDtypeStruct((degrees, 8, L), f32),
        ),
        in_specs=[vmem, anywhere, vmem, vmem, vmem, smem, smem],
        out_specs=(vmem, vmem, vmem),
        scratch_shapes=[
            pltpu.VMEM((8, K, N), bf16),
            pltpu.VMEM((Q, 8 * D, N), bf16),
            pltpu.VMEM((Q, 8 * D, N), bf16),
            pltpu.VMEM((Q, 2, N), jnp.int32),
            pltpu.VMEM((Q, 2, S, N), bf16),
            pltpu.VMEM((2, 8 * D, S), bf16),
            pltpu.VMEM((2, S // 128, 8 * D, 128), f32),
            pltpu.VMEM((Z, 8, L), f32),
            pltpu.VMEM((ITERS, Z, 8, L), f32),
            pltpu.VMEM((Q, 2, 8 * D, N), f32),
            pltpu.VMEM((Q, 8 * D, N), f32),
            pltpu.VMEM((2, 2, 8 * D, N), bf16),
            pltpu.VMEM((ITERS, Q, 8, N), f32),
            pltpu.VMEM((ITERS, Q, 8, N), f32),
            pltpu.VMEM((ITERS, Q, 8, N), f32),
            pltpu.VMEM((S // 128, 8 * D, 128), f32),
            pltpu.VMEM((ITERS, Z, 8, L), f32),
            pltpu.VMEM((ITERS, Z, 8, L), f32),
            pltpu.VMEM((F, 8, L), f32),
            pltpu.VMEM((F, 8, L), f32),
            pltpu.VMEM((ITERS, F, 8, L), f32),
            pltpu.VMEM((F, 8, L), f32),
            pltpu.VMEM((8, L), f32),
            pltpu.VMEM((ITERS, F * T, 8, 128), f32),
            dma, dma((Q,)), dma((Q,)), dma((Q,)), dma((Q,)), dma((Z,)), dma((Z,)),
            dma((ITERS, Z)), dma((ITERS, Z)), dma((ITERS, Q)), dma((ITERS, Q)), dma((ITERS, Q)), dma((ITERS, Q)),
            dma((ITERS, Z)), dma((ITERS, Z)),
            dma((2, F)), dma((2, F)), dma((ITERS, F)), dma((ITERS, F)), dma((ITERS,)), dma((ITERS,)),
        ],
        compiler_params=pltpu.CompilerParams(
            collective_id=0, has_side_effects=True, vmem_limit_bytes=48 * 1024 * 1024),
        cost_estimate=pl.CostEstimate(flops=10**10, bytes_accessed=10**7, transcendentals=0),
    )(visibilities[0, 0], coherency[0, 0], stations[0], jones[0], dual[0], cluster, rho_table)
    return jones_out[None], dual_out[None], poly


def solution(mesh):
    return jax.shard_map(
        body,
        mesh=mesh,
        in_specs=(
            P("tm", "freq", None, None),
            P("tm", "freq", None, None, None),
            P("tm", None, None),
            P("freq", None, "tm"),
            P("freq", None, "tm"),
            P(),
            P(),
        ),
        out_specs=(P("freq", None, "tm"), P("freq", None, "tm"), P(None, None, "tm")),
        check_vma=False,
    )
```

```python
import functools
import math

import jax
import jax.numpy as jnp
import numpy as np
from jax import lax
from jax.experimental import pallas as pl
from jax.experimental.pallas import tpu as pltpu
from jax.sharding import PartitionSpec as P

ITERS = 2
MESH = pl.DeviceIdType.MESH
ROWS = 8

step_size = 0.5
epsilon = 1e-06


def poly_basis(channels, degrees):
    points = np.linspace(-1.0, 1.0, channels)
    columns = []
    for degree in range(degrees):
        column = points**degree
        for earlier in columns:
            column = column - np.dot(earlier, column) * earlier
        column = column / np.sqrt(np.dot(column, column))
        columns.append(column)
    return np.stack(columns, axis=1).astype(np.float32)


def split_entries(parts):
    return [[(parts[4 * i + 2 * j], parts[4 * i + 2 * j + 1]) for j in range(2)] for i in range(2)]


def join_entries(mat):
    return [part for row in mat for entry in row for part in entry]


def times_pair(a, b):
    return (a[0] * b[0] - a[1] * b[1], a[0] * b[1] + a[1] * b[0])


def times_conj(a, b):
    return (a[0] * b[0] + a[1] * b[1], a[1] * b[0] - a[0] * b[1])


def add_pairs(a, b):
    return (a[0] + b[0], a[1] + b[1])


def mat_mul(a, b):
    return [[add_pairs(times_pair(a[i][0], b[0][j]), times_pair(a[i][1], b[1][j])) for j in range(2)] for i in range(2)]


def mat_mul_right_h(a, b):
    return [[add_pairs(times_conj(a[i][0], b[j][0]), times_conj(a[i][1], b[j][1])) for j in range(2)] for i in range(2)]


def mat_mul_left_h(a, b):
    return [[add_pairs(times_conj(b[0][j], a[0][i]), times_conj(b[1][j], a[1][i])) for j in range(2)] for i in range(2)]


def kernel(
    T, F, Z, nd, S, K, N, basis, weight,
    vis_hbm, coh_hbm, st_hbm, jones_hbm, dual_hbm, cluster_ref, table_ref,
    jones_out, dual_out, poly_out,
    vis_ref, coh_raw, coh_out, coh_in, st_all, oh, tab, tabs, gz, zde, gp, abuf, xbuf, partial, part_in, res, acc, gout, gin,
    jn, du, de, fit, rho, sq,
    raw_sem, st_ss, st_rs, coh_ss, coh_rs, gz_ss, gz_rs, zd_ss, zd_rs, pa_ss, pa_rs, re_ss, re_rs, go_ss, go_rs,
    in_ss, in_rs, de_ss, de_rs, sq_ss, sq_rs,
):
    me = lax.axis_index("tm")
    fi = lax.axis_index("freq")
    Q = T // Z
    z, q = me // Q, lax.rem(me, Q)
    D = Z * nd
    tiles = D // ROWS
    g = ROWS // nd
    L = nd * S
    lane_tiles = S // 128
    half = S // 2
    degrees = basis.shape[1]

    def remote(src, dst, send, recv, to):
        return pltpu.make_async_remote_copy(
            src_ref=src, dst_ref=dst, send_sem=send, recv_sem=recv, device_id=to, device_id_type=MESH)

    def plane(u):
        return {"tm": z * Q + u}

    def column(v):
        return {"tm": v * Q + q}

    def st_copy(src, to):
        return remote(st_all.at[src], st_all.at[src], st_ss.at[to], st_rs.at[src], plane(to))

    def coh_copy(src, to):
        return remote(coh_out.at[to], coh_in.at[src], coh_ss.at[to], coh_rs.at[src], plane(to))

    def part_copy(it, src, to):
        return remote(partial.at[it, to], part_in.at[it, src], pa_ss.at[it, to], pa_rs.at[it, src], plane(to))

    def res_copy(it, src, to):
        return remote(res.at[it, src], res.at[it, src], re_ss.at[it, to], re_rs.at[it, src], plane(to))

    def gz_copy(src, to):
        return remote(gz.at[src], gz.at[src], gz_ss.at[to], gz_rs.at[src], column(to))

    def zd_copy(it, src, to):
        return remote(de.at[it, fi], zde.at[it, src], zd_ss.at[it, to], zd_rs.at[it, src], column(to))

    def go_copy(it, h, src, to):
        return remote(gout.at[it, h, to], gin.at[it, h, src], go_ss.at[it, h, to], go_rs.at[it, h, src], column(to))

    def state_copy(which, src, to):
        ref = (jn, du)[which]
        return remote(ref.at[src], ref.at[src], in_ss.at[which, to], in_rs.at[which, src], {"freq": to})

    def de_copy(it, src, to):
        return remote(de.at[it, src], de.at[it, src], de_ss.at[it, to], de_rs.at[it, src], {"freq": to})

    def sq_copy(it, to_f, to_t):
        mine = fi * T + me
        return remote(sq.at[it, mine], sq.at[it, mine], sq_ss.at[it], sq_rs.at[it], {"tm": to_t, "freq": to_f})

    def sq_all(it):
        span = sq.at[it, pl.ds(0, F * T - 1)]
        return remote(span, span, sq_ss.at[it], sq_rs.at[it], {"tm": me, "freq": fi})

    def each_other(fn):
        def one(o, _):
            fn(lax.rem(fi * T + me + o, F * T))
            return 0
        lax.fori_loop(1, F * T, one, 0)

    plane_next = [lax.rem(q + o, Q) for o in range(1, Q)]
    plane_from = [lax.rem(q - o + Q, Q) for o in range(1, Q)]
    column_others = [lax.rem(z + o, Z) for o in range(1, Z)]
    freq_others = [lax.rem(fi + o, F) for o in range(1, F)]

    jones_in = pltpu.make_async_copy(jones_hbm, jn.at[fi], raw_sem.at[0])
    st_in = pltpu.make_async_copy(st_hbm, st_all.at[q], raw_sem.at[1])
    raw = pltpu.make_async_copy(coh_hbm, coh_raw, raw_sem.at[2])
    dual_in = pltpu.make_async_copy(dual_hbm, du.at[fi], raw_sem.at[3])
    vis_in = pltpu.make_async_copy(vis_hbm, vis_ref, raw_sem.at[4])
    for copy in (jones_in, st_in, raw, dual_in, vis_in):
        copy.start()
    barrier = pltpu.get_barrier_semaphore()

    def greet(d):
        pl.semaphore_signal(barrier, inc=1, device_id={"tm": lax.rem(d, T), "freq": d // T}, device_id_type=MESH)

    each_other(greet)
    jones_in.wait()
    gz[z] = jn[fi]
    st_in.wait()
    for d in range(nd):
        value = table_ref[cluster_ref[me * nd + d]]
        rho[:, d * S:(d + 1) * S] = jnp.full((ROWS, S), value, jnp.float32)
    pl.semaphore_wait(barrier, F * T - 1)

    for to in plane_next:
        st_copy(q, to).start()
    for to in column_others:
        gz_copy(z, to).start()
    raw.wait()

    slot = lax.broadcasted_iota(jnp.int32, (ROWS, N), 0) // nd
    for c in range(8):
        full = coh_raw[c].astype(jnp.float32)
        for u in range(Q):
            rows = []
            for m in range(tiles):
                out = None
                for s in range(g):
                    unit = (m * g + s) * Q + u
                    tile = full[8 * (unit // g):8 * (unit // g) + 8, :]
                    shift = ((s - unit % g) % g) * nd
                    if shift:
                        tile = pltpu.roll(tile, shift, 0)
                    out = tile if s == 0 else jnp.where(slot == s, tile, out)
                rows.append(out)
            block = rows[0] if tiles == 1 else jnp.concatenate(rows, axis=0)
            coh_out[u, c * D:(c + 1) * D, :] = block.astype(jnp.bfloat16)
    for to in plane_next:
        coh_copy(q, to).start()
    coh_in[q] = coh_out[q]
    dual_in.wait()
    vis_in.wait()
    for to in freq_others:
        state_copy(0, fi, to).start()
        state_copy(1, fi, to).start()

    def build(i, _):
        u = lax.rem(q - i + Q, Q)

        @pl.when(u != q)
        def _():
            st_copy(u, q).wait_recv()
        for e in range(2):
            row = st_all[u, e:e + 1, :]
            for lo in range(0, S, 64):
                ids = lax.broadcasted_iota(jnp.int32, (64, N), 0) + lo
                oh[u, lo:lo + 64, e * N:(e + 1) * N] = jnp.where(ids == row, 1.0, 0.0).astype(jnp.bfloat16)
        return 0

    lax.fori_loop(0, Q, build, 0)

    def set_table():
        for v in range(Z):
            now = gz[v]
            for d in range(nd):
                piece = now[:, d * S:(d + 1) * S]
                high = piece.astype(jnp.bfloat16).astype(jnp.float32)
                low = piece - high
                for k in range(lane_tiles):
                    lanes = slice(k * 128, (k + 1) * 128)
                    tabs[0, k, pl.ds(v * nd + d, 8, stride=D), :] = high[:, lanes]
                    tabs[1, k, pl.ds(v * nd + d, 8, stride=D), :] = low[:, lanes]
        for h in range(2):
            for k in range(lane_tiles):
                tab[h * 8 * D:(h + 1) * 8 * D, k * 128:(k + 1) * 128] = tabs[h, k].astype(jnp.bfloat16)

    def gather_time(u):
        for e in range(2):
            got = jnp.dot(tab[...], oh[u, :, e * N:(e + 1) * N], preferred_element_type=jnp.float32)
            gp[u, e] = got[:8 * D] + got[8 * D:]

    def tile_rows(c, m):
        return slice(c * D + m * ROWS, c * D + (m + 1) * ROWS)

    def sky_tiles(u, lanes):
        sky = [coh_in[u, c * D:(c + 1) * D, lanes].astype(jnp.float32) for c in range(8)]
        return [split_entries([part[m * ROWS:(m + 1) * ROWS] for part in sky]) for m in range(tiles)]

    def forward_time(it, u):
        for lo in range(0, N, 128):
            lanes = slice(lo, lo + 128)
            sky = sky_tiles(u, lanes)
            sums = None
            for m in range(tiles):
                first = split_entries([gp[u, 0, tile_rows(c, m), lanes] for c in range(8)])
                second = split_entries([gp[u, 1, tile_rows(c, m), lanes] for c in range(8)])
                prod = mat_mul(first, sky[m])
                for c, part in enumerate(join_entries(prod)):
                    abuf[u, tile_rows(c, m), lanes] = part
                model = join_entries(mat_mul_right_h(prod, second))
                sums = model if sums is None else [x + y for x, y in zip(sums, model)]
            for c in range(8):
                partial[it, u, c:c + 1, lanes] = jnp.sum(sums[c], axis=0, keepdims=True)

        @pl.when(u != q)
        def _():
            part_copy(it, q, u).start()

    def backward_time(it, u):
        @pl.when(u != q)
        def _():
            res_copy(it, u, q).wait_recv()
        for lo in range(0, N, 128):
            lanes = slice(lo, lo + 128)
            sky = sky_tiles(u, lanes)
            resid = split_entries([
                jnp.broadcast_to(res[it, u, c:c + 1, lanes], (ROWS, 128)) for c in range(8)])
            grads = [[None] * (8 * tiles), [None] * (8 * tiles)]
            for m in range(tiles):
                prod = split_entries([abuf[u, tile_rows(c, m), lanes] for c in range(8)])
                second = split_entries([gp[u, 1, tile_rows(c, m), lanes] for c in range(8)])
                first_grad = join_entries(mat_mul(resid, mat_mul_right_h(second, sky[m])))
                second_grad = join_entries(mat_mul_left_h(resid, prod))
                for c in range(8):
                    grads[0][c * tiles + m] = first_grad[c]
                    grads[1][c * tiles + m] = second_grad[c]
            for e in range(2):
                for pair in range(4 * tiles):
                    both = jnp.concatenate(grads[e][2 * pair:2 * pair + 2], axis=0)
                    high = both.astype(jnp.bfloat16)
                    low = (both - high.astype(jnp.float32)).astype(jnp.bfloat16)
                    here = slice(e * N + lo, e * N + lo + 128)
                    xbuf[u, 16 * pair:16 * pair + 16, here] = high
                    xbuf[u, 8 * D + 16 * pair:8 * D + 16 * pair + 16, here] = low

    def scatter_half(it, h):
        def add_time(u, total):
            return total + lax.dot_general(
                xbuf[u], oh[u, h * half:(h + 1) * half, :], (((1,), (1,)), ((), ())),
                preferred_element_type=jnp.float32)

        total = lax.fori_loop(0, Q, add_time, jnp.zeros((16 * D, half), jnp.float32))
        total = total[:8 * D] + total[8 * D:]
        for k in range(half // 128):
            acc[h, k] = total[:, k * 128:(k + 1) * 128]
        for v in range(Z):
            for d in range(nd):
                for k in range(half // 128):
                    gout[it, h, v, :, d * half + k * 128:d * half + (k + 1) * 128] = (
                        acc[h, k, pl.ds(v * nd + d, 8, stride=D), :])
        for v in column_others:
            go_copy(it, h, z, v).start()

    def consensus():
        sums = [jn[f] + du[f] / rho[...] for f in range(F)]
        for j in range(degrees):
            total = None
            for f in range(F):
                term = float(basis[f, j]) * sums[f]
                total = term if total is None else total + term
            poly_out[j] = total
        for f in range(F):
            total = None
            for j in range(degrees):
                term = float(basis[f, j]) * poly_out[j]
                total = term if total is None else total + term
            fit[f] = total

    for v in column_others:
        gz_copy(v, z).wait_recv()

    for it in range(ITERS):
        set_table()
        if it == 0:
            def gather_step(i, _):
                gather_time(lax.rem(q - i + Q, Q))
                return 0

            def forward_step(i, _):
                u = lax.rem(q - i + Q, Q)

                @pl.when(u != q)
                def _():
                    coh_copy(u, q).wait_recv()
                forward_time(it, u)
                return 0

            lax.fori_loop(0, Q, gather_step, 0)
            lax.fori_loop(0, Q, forward_step, 0)
            for f in freq_others:
                state_copy(0, f, fi).wait_recv()
                state_copy(1, f, fi).wait_recv()
            consensus()
        else:
            def both_step(i, _):
                u = lax.rem(q + 1 + i, Q)
                gather_time(u)
                forward_time(it, u)
                return 0

            lax.fori_loop(0, Q, both_step, 0)

        model = partial[it, q]
        for u in plane_from:
            part_copy(it, u, q).wait_recv()
            model = model + part_in[it, u]
        res[it, q] = weight * (model - vis_ref[...])
        for to in plane_next:
            res_copy(it, q, to).start()

        def backward_step(i, _):
            backward_time(it, lax.rem(q - i + Q, Q))
            return 0

        lax.fori_loop(0, Q, backward_step, 0)

        for h in range(2):
            scatter_half(it, h)
        for h in range(2):
            grad = gout[it, h, z]
            for v in column_others:
                go_copy(it, h, v, z).wait_recv()
                grad = grad + gin[it, h, v]
            for d in range(nd):
                de[it, fi, :, d * S + h * half:d * S + (h + 1) * half] = grad[:, d * half:(d + 1) * half]
        descent = de[it, fi] + du[fi] + rho[...] * (jn[fi] - fit[fi])
        de[it, fi] = descent
        squares = descent * descent
        total = squares[:, 0:128]
        for lo in range(128, L, 128):
            total = total + squares[:, lo:lo + 128]
        sq[it, fi * T + me] = total
        last = it + 1 == ITERS
        if not last:
            for v in column_others:
                zd_copy(it, z, v).start()
        for f in freq_others:
            de_copy(it, fi, f).start()
        each_other(lambda d: sq_copy(it, d // T, lax.rem(d, T)).start())
        sq_all(it).wait_recv()
        for f in freq_others:
            de_copy(it, f, fi).wait_recv()
        if it == 0:
            for f in freq_others:
                state_copy(0, fi, f).wait_send()
                state_copy(1, fi, f).wait_send()
            for v in column_others:
                gz_copy(z, v).wait_send()
        scales = []
        for f in range(F):
            tile = jnp.sum(sq[it, pl.ds(f * T, T)], axis=0)
            whole = jnp.sum(jnp.sum(tile, axis=1, keepdims=True), axis=0, keepdims=True)
            scale = jnp.sqrt(whole / (8.0 * K * S) + epsilon)
            scales.append(scale)
            jn[f] = jn[f] - step_size * de[it, f] / scale
        consensus()
        for f in range(F):
            du[f] = du[f] + rho[...] * (jn[f] - fit[f])
        if not last:
            own = scales[0]
            for f in range(1, F):
                own = jnp.where(fi == f, scales[f], own)
            gz[z] = jn[fi]
            for v in column_others:
                zd_copy(it, v, z).wait_recv()
                gz[v] = gz[v] - step_size * zde[it, v] / own

    jones_out[...] = jn[fi]
    dual_out[...] = du[fi]
    for to in plane_next:
        st_copy(q, to).wait_send()
        coh_copy(q, to).wait_send()
        for it in range(ITERS):
            part_copy(it, q, to).wait_send()
            res_copy(it, q, to).wait_send()
    for it in range(ITERS):
        for v in column_others:
            go_copy(it, 0, z, v).wait_send()
            go_copy(it, 1, z, v).wait_send()
            if it + 1 < ITERS:
                zd_copy(it, z, v).wait_send()
        sq_all(it).wait_send()
        for f in freq_others:
            de_copy(it, fi, f).wait_send()


def body(visibilities, coherency, stations, jones, dual, cluster, rho_table):
    T = lax.axis_size("tm")
    F = lax.axis_size("freq")
    K, N = coherency.shape[3], coherency.shape[4]
    L = jones.shape[2]
    nd = K // T
    S = L // nd
    Z = ROWS // nd
    Q = T // Z
    D = Z * nd
    basis = poly_basis(F, min(3, F - 1))
    degrees = basis.shape[1]
    weight = np.float32(math.sqrt(S / (2.0 * T * N)))
    vmem = pl.BlockSpec(memory_space=pltpu.VMEM)
    smem = pl.BlockSpec(memory_space=pltpu.SMEM)
    anywhere = pl.BlockSpec(memory_space=pl.ANY)
    f32, bf16 = jnp.float32, jnp.bfloat16
    dma = pltpu.SemaphoreType.DMA
    jones_out, dual_out, poly = pl.pallas_call(
        functools.partial(kernel, T, F, Z, nd, S, K, N, basis, weight),
        out_shape=(
            jax.ShapeDtypeStruct((8, L), f32),
            jax.ShapeDtypeStruct((8, L), f32),
            jax.ShapeDtypeStruct((degrees, 8, L), f32),
        ),
        in_specs=[anywhere] * 5 + [smem] * 2,
        out_specs=(vmem, vmem, vmem),
        scratch_shapes=[
            pltpu.VMEM((8, N), f32),
            pltpu.VMEM((8, K, N), bf16),
            pltpu.VMEM((Q, 8 * D, N), bf16),
            pltpu.VMEM((Q, 8 * D, N), bf16),
            pltpu.VMEM((Q, 2, N), jnp.int32),
            pltpu.VMEM((Q, S, 2 * N), bf16),
            pltpu.VMEM((16 * D, S), bf16),
            pltpu.VMEM((2, S // 128, 8 * D, 128), f32),
            pltpu.VMEM((Z, 8, L), f32),
            pltpu.VMEM((ITERS, Z, 8, L), f32),
            pltpu.VMEM((Q, 2, 8 * D, N), f32),
            pltpu.VMEM((Q, 8 * D, N), f32),
            pltpu.VMEM((Q, 16 * D, 2 * N), bf16),
            pltpu.VMEM((ITERS, Q, 8, N), f32),
            pltpu.VMEM((ITERS, Q, 8, N), f32),
            pltpu.VMEM((ITERS, Q, 8, N), f32),
            pltpu.VMEM((2, S // 256, 8 * D, 128), f32),
            pltpu.VMEM((ITERS, 2, Z, 8, L // 2), f32),
            pltpu.VMEM((ITERS, 2, Z, 8, L // 2), f32),
            pltpu.VMEM((F, 8, L), f32),
            pltpu.VMEM((F, 8, L), f32),
            pltpu.VMEM((ITERS, F, 8, L), f32),
            pltpu.VMEM((F, 8, L), f32),
            pltpu.VMEM((8, L), f32),
            pltpu.VMEM((ITERS, F * T, 8, 128), f32),
            dma((5,)), dma((Q,)), dma((Q,)), dma((Q,)), dma((Q,)), dma((Z,)), dma((Z,)),
            dma((ITERS, Z)), dma((ITERS, Z)), dma((ITERS, Q)), dma((ITERS, Q)), dma((ITERS, Q)), dma((ITERS, Q)),
            dma((ITERS, 2, Z)), dma((ITERS, 2, Z)),
            dma((2, F)), dma((2, F)), dma((ITERS, F)), dma((ITERS, F)), dma((ITERS,)), dma((ITERS,)),
        ],
        compiler_params=pltpu.CompilerParams(
            collective_id=0, has_side_effects=True, vmem_limit_bytes=60 * 1024 * 1024),
        cost_estimate=pl.CostEstimate(flops=10**10, bytes_accessed=10**7, transcendentals=0),
    )(visibilities[0, 0], coherency[0, 0], stations[0], jones[0], dual[0], cluster, rho_table)
    return jones_out[None], dual_out[None], poly


def solution(mesh):
    return jax.shard_map(
        body,
        mesh=mesh,
        in_specs=(
            P("tm", "freq", None, None),
            P("tm", "freq", None, None, None),
            P("tm", None, None),
            P("freq", None, "tm"),
            P("freq", None, "tm"),
            P(),
            P(),
        ),
        out_specs=(P("freq", None, "tm"), P("freq", None, "tm"), P(None, None, "tm")),
        check_vma=False,
    )
```

```python
import functools
import math

import jax
import jax.numpy as jnp
import numpy as np
from jax import lax
from jax.experimental import pallas as pl
from jax.experimental.pallas import tpu as pltpu
from jax.sharding import PartitionSpec as P

ITERS = 2
MESH = pl.DeviceIdType.MESH
ROWS = 8

step_size = 0.5
epsilon = 1e-06


def poly_basis(channels, degrees):
    points = np.linspace(-1.0, 1.0, channels)
    columns = []
    for degree in range(degrees):
        column = points**degree
        for earlier in columns:
            column = column - np.dot(earlier, column) * earlier
        column = column / np.sqrt(np.dot(column, column))
        columns.append(column)
    return np.stack(columns, axis=1).astype(np.float32)


def split_entries(parts):
    return [[(parts[4 * i + 2 * j], parts[4 * i + 2 * j + 1]) for j in range(2)] for i in range(2)]


def join_entries(mat):
    return [part for row in mat for entry in row for part in entry]


def times_pair(a, b):
    return (a[0] * b[0] - a[1] * b[1], a[0] * b[1] + a[1] * b[0])


def times_conj(a, b):
    return (a[0] * b[0] + a[1] * b[1], a[1] * b[0] - a[0] * b[1])


def add_pairs(a, b):
    return (a[0] + b[0], a[1] + b[1])


def mat_mul(a, b):
    return [[add_pairs(times_pair(a[i][0], b[0][j]), times_pair(a[i][1], b[1][j])) for j in range(2)] for i in range(2)]


def mat_mul_right_h(a, b):
    return [[add_pairs(times_conj(a[i][0], b[j][0]), times_conj(a[i][1], b[j][1])) for j in range(2)] for i in range(2)]


def mat_mul_left_h(a, b):
    return [[add_pairs(times_conj(b[0][j], a[0][i]), times_conj(b[1][j], a[1][i])) for j in range(2)] for i in range(2)]


def kernel(
    T, F, Z, nd, S, K, N, basis, weight,
    vis_hbm, coh_hbm, st_hbm, jones_hbm, dual_hbm, cluster_ref, table_ref,
    jones_out, dual_out, poly_out,
    vis_all, coh_raw, coh_out, coh_in, st_all, oh, tab, tabs, gz, zde, gp, abuf, xbuf, partial, part_in, res, acc, gout, gin,
    jn, du, de, fit, rho, sq, sqs,
    raw_sem, vi_ss, vi_rs, st_ss, st_rs, coh_ss, coh_rs, gz_ss, gz_rs, zd_ss, zd_rs, pa_ss, pa_rs, go_ss, go_rs,
    in_ss, in_rs, de_ss, de_rs, sq_ss, sq_rs, ss_ss, ss_rs,
):
    me = lax.axis_index("tm")
    fi = lax.axis_index("freq")
    Q = T // Z
    z, q = me // Q, lax.rem(me, Q)
    D = Z * nd
    tiles = D // ROWS
    g = ROWS // nd
    L = nd * S
    lane_tiles = S // 128
    half = S // 2
    degrees = basis.shape[1]

    def remote(src, dst, send, recv, to):
        return pltpu.make_async_remote_copy(
            src_ref=src, dst_ref=dst, send_sem=send, recv_sem=recv, device_id=to, device_id_type=MESH)

    def plane(u):
        return {"tm": z * Q + u}

    def column(v):
        return {"tm": v * Q + q}

    def st_copy(src, to):
        return remote(st_all.at[src], st_all.at[src], st_ss.at[to], st_rs.at[src], plane(to))

    def coh_copy(src, to):
        return remote(coh_out.at[to], coh_in.at[src], coh_ss.at[to], coh_rs.at[src], plane(to))

    def vis_copy(src, to):
        return remote(vis_all.at[src], vis_all.at[src], vi_ss.at[to], vi_rs.at[src], plane(to))

    def part_copy(it, u, src, to):
        return remote(
            partial.at[it, u], part_in.at[it, u, src], pa_ss.at[it, u, to], pa_rs.at[it, u, src], plane(to))

    def gz_copy(src, to):
        return remote(gz.at[src], gz.at[src], gz_ss.at[to], gz_rs.at[src], column(to))

    def zd_copy(it, src, to):
        return remote(de.at[it, fi], zde.at[it, src], zd_ss.at[it, to], zd_rs.at[it, src], column(to))

    def go_copy(it, h, src, to):
        return remote(gout.at[it, h, to], gin.at[it, h, src], go_ss.at[it, h, to], go_rs.at[it, h, src], column(to))

    def state_copy(which, src, to):
        ref = (jn, du)[which]
        return remote(ref.at[src], ref.at[src], in_ss.at[which, to], in_rs.at[which, src], {"freq": to})

    def de_copy(it, src, to):
        return remote(de.at[it, src], de.at[it, src], de_ss.at[it, to], de_rs.at[it, src], {"freq": to})

    def sq_copy(it, to):
        return remote(sq.at[it, q], sq.at[it, q], sq_ss.at[it], sq_rs.at[it], plane(to))

    def sq_all(it):
        span = sq.at[it, pl.ds(0, Q - 1)]
        return remote(span, span, sq_ss.at[it], sq_rs.at[it], plane(q))

    def sums_copy(it, to_f, to_v):
        mine = fi * Z + z
        return remote(
            sqs.at[it, mine], sqs.at[it, mine], ss_ss.at[it], ss_rs.at[it], {"tm": to_v * Q + q, "freq": to_f})

    def sums_all(it):
        span = sqs.at[it, pl.ds(0, F * Z - 1)]
        return remote(span, span, ss_ss.at[it], ss_rs.at[it], {"tm": me, "freq": fi})

    def each_other(fn):
        def one(o, _):
            other = lax.rem(fi * Z + z + o, F * Z)
            fn(other // Z, lax.rem(other, Z))
            return 0
        lax.fori_loop(1, F * Z, one, 0)

    plane_next = [lax.rem(q + o, Q) for o in range(1, Q)]
    plane_from = [lax.rem(q - o + Q, Q) for o in range(1, Q)]
    column_others = [lax.rem(z + o, Z) for o in range(1, Z)]
    freq_others = [lax.rem(fi + o, F) for o in range(1, F)]

    jones_in = pltpu.make_async_copy(jones_hbm, jn.at[fi], raw_sem.at[0])
    st_in = pltpu.make_async_copy(st_hbm, st_all.at[q], raw_sem.at[1])
    raw = pltpu.make_async_copy(coh_hbm, coh_raw, raw_sem.at[2])
    dual_in = pltpu.make_async_copy(dual_hbm, du.at[fi], raw_sem.at[3])
    vis_in = pltpu.make_async_copy(vis_hbm, vis_all.at[q], raw_sem.at[4])
    for copy in (jones_in, st_in, raw, dual_in, vis_in):
        copy.start()
    barrier = pltpu.get_barrier_semaphore()

    for u in plane_next:
        pl.semaphore_signal(barrier, inc=1, device_id=plane(u), device_id_type=MESH)
    each_other(lambda f, v: pl.semaphore_signal(
        barrier, inc=1, device_id={"tm": v * Q + q, "freq": f}, device_id_type=MESH))
    jones_in.wait()
    gz[z] = jn[fi]
    st_in.wait()
    for d in range(nd):
        value = table_ref[cluster_ref[me * nd + d]]
        rho[:, d * S:(d + 1) * S] = jnp.full((ROWS, S), value, jnp.float32)
    pl.semaphore_wait(barrier, Q - 1 + F * Z - 1)

    for to in plane_next:
        st_copy(q, to).start()
    for to in column_others:
        gz_copy(z, to).start()
    raw.wait()

    slot = lax.broadcasted_iota(jnp.int32, (ROWS, N), 0) // nd
    for c in range(8):
        full = coh_raw[c].astype(jnp.float32)
        for u in range(Q):
            rows = []
            for m in range(tiles):
                out = None
                for s in range(g):
                    unit = (m * g + s) * Q + u
                    tile = full[8 * (unit // g):8 * (unit // g) + 8, :]
                    shift = ((s - unit % g) % g) * nd
                    if shift:
                        tile = pltpu.roll(tile, shift, 0)
                    out = tile if s == 0 else jnp.where(slot == s, tile, out)
                rows.append(out)
            block = rows[0] if tiles == 1 else jnp.concatenate(rows, axis=0)
            coh_out[u, c * D:(c + 1) * D, :] = block.astype(jnp.bfloat16)
    for to in plane_next:
        coh_copy(q, to).start()
    coh_in[q] = coh_out[q]
    dual_in.wait()
    vis_in.wait()
    for to in plane_next:
        vis_copy(q, to).start()
    for to in freq_others:
        state_copy(0, fi, to).start()
        state_copy(1, fi, to).start()

    def build(i, _):
        u = lax.rem(q - i + Q, Q)

        @pl.when(u != q)
        def _():
            st_copy(u, q).wait_recv()
        for e in range(2):
            row = st_all[u, e:e + 1, :]
            for lo in range(0, S, 64):
                ids = lax.broadcasted_iota(jnp.int32, (64, N), 0) + lo
                oh[u, lo:lo + 64, e * N:(e + 1) * N] = jnp.where(ids == row, 1.0, 0.0).astype(jnp.bfloat16)
        return 0

    lax.fori_loop(0, Q, build, 0)

    def set_table():
        for v in range(Z):
            now = gz[v]
            for d in range(nd):
                piece = now[:, d * S:(d + 1) * S]
                high = piece.astype(jnp.bfloat16).astype(jnp.float32)
                low = piece - high
                for k in range(lane_tiles):
                    lanes = slice(k * 128, (k + 1) * 128)
                    tabs[0, k, pl.ds(v * nd + d, 8, stride=D), :] = high[:, lanes]
                    tabs[1, k, pl.ds(v * nd + d, 8, stride=D), :] = low[:, lanes]
        for h in range(2):
            for k in range(lane_tiles):
                tab[h * 8 * D:(h + 1) * 8 * D, k * 128:(k + 1) * 128] = tabs[h, k].astype(jnp.bfloat16)

    def gather_time(u):
        for e in range(2):
            got = jnp.dot(tab[...], oh[u, :, e * N:(e + 1) * N], preferred_element_type=jnp.float32)
            gp[u, e] = got[:8 * D] + got[8 * D:]

    def tile_rows(c, m):
        return slice(c * D + m * ROWS, c * D + (m + 1) * ROWS)

    def sky_tiles(u, lanes):
        sky = [coh_in[u, c * D:(c + 1) * D, lanes].astype(jnp.float32) for c in range(8)]
        return [split_entries([part[m * ROWS:(m + 1) * ROWS] for part in sky]) for m in range(tiles)]

    def forward_time(it, u):
        for lo in range(0, N, 128):
            lanes = slice(lo, lo + 128)
            sky = sky_tiles(u, lanes)
            sums = None
            for m in range(tiles):
                first = split_entries([gp[u, 0, tile_rows(c, m), lanes] for c in range(8)])
                second = split_entries([gp[u, 1, tile_rows(c, m), lanes] for c in range(8)])
                prod = mat_mul(first, sky[m])
                for c, part in enumerate(join_entries(prod)):
                    abuf[u, tile_rows(c, m), lanes] = part
                model = join_entries(mat_mul_right_h(prod, second))
                sums = model if sums is None else [x + y for x, y in zip(sums, model)]
            for c in range(8):
                partial[it, u, c:c + 1, lanes] = jnp.sum(sums[c], axis=0, keepdims=True)

        for to in plane_next:
            part_copy(it, u, q, to).start()

    def backward_time(it, u):
        if it == 0:
            @pl.when(u != q)
            def _():
                vis_copy(u, q).wait_recv()
        model = partial[it, u]
        for src in plane_from:
            part_copy(it, u, src, q).wait_recv()
            model = model + part_in[it, u, src]
        res[u] = weight * (model - vis_all[u])
        for lo in range(0, N, 128):
            lanes = slice(lo, lo + 128)
            sky = sky_tiles(u, lanes)
            resid = split_entries([
                jnp.broadcast_to(res[u, c:c + 1, lanes], (ROWS, 128)) for c in range(8)])
            grads = [[None] * (8 * tiles), [None] * (8 * tiles)]
            for m in range(tiles):
                prod = split_entries([abuf[u, tile_rows(c, m), lanes] for c in range(8)])
                second = split_entries([gp[u, 1, tile_rows(c, m), lanes] for c in range(8)])
                first_grad = join_entries(mat_mul(resid, mat_mul_right_h(second, sky[m])))
                second_grad = join_entries(mat_mul_left_h(resid, prod))
                for c in range(8):
                    grads[0][c * tiles + m] = first_grad[c]
                    grads[1][c * tiles + m] = second_grad[c]
            for e in range(2):
                for pair in range(4 * tiles):
                    both = jnp.concatenate(grads[e][2 * pair:2 * pair + 2], axis=0)
                    high = both.astype(jnp.bfloat16)
                    low = (both - high.astype(jnp.float32)).astype(jnp.bfloat16)
                    here = slice(e * N + lo, e * N + lo + 128)
                    xbuf[u, 16 * pair:16 * pair + 16, here] = high
                    xbuf[u, 8 * D + 16 * pair:8 * D + 16 * pair + 16, here] = low

    def scatter_half(it, h):
        def add_time(u, total):
            return total + lax.dot_general(
                xbuf[u], oh[u, h * half:(h + 1) * half, :], (((1,), (1,)), ((), ())),
                preferred_element_type=jnp.float32)

        total = lax.fori_loop(0, Q, add_time, jnp.zeros((16 * D, half), jnp.float32))
        total = total[:8 * D] + total[8 * D:]
        for k in range(half // 128):
            acc[h, k] = total[:, k * 128:(k + 1) * 128]
        for v in range(Z):
            for d in range(nd):
                for k in range(half // 128):
                    gout[it, h, v, :, d * half + k * 128:d * half + (k + 1) * 128] = (
                        acc[h, k, pl.ds(v * nd + d, 8, stride=D), :])
        for v in column_others:
            go_copy(it, h, z, v).start()

    def consensus():
        sums = [jn[f] + du[f] / rho[...] for f in range(F)]
        for j in range(degrees):
            total = None
            for f in range(F):
                term = float(basis[f, j]) * sums[f]
                total = term if total is None else total + term
            poly_out[j] = total
        for f in range(F):
            total = None
            for j in range(degrees):
                term = float(basis[f, j]) * poly_out[j]
                total = term if total is None else total + term
            fit[f] = total

    for v in column_others:
        gz_copy(v, z).wait_recv()

    for it in range(ITERS):
        set_table()
        if it == 0:
            def gather_step(i, _):
                gather_time(i)
                return 0

            def forward_step(i, _):
                @pl.when(i != q)
                def _():
                    coh_copy(i, q).wait_recv()
                forward_time(it, i)
                return 0

            lax.fori_loop(0, Q, gather_step, 0)
            lax.fori_loop(0, Q, forward_step, 0)
            for f in freq_others:
                state_copy(0, f, fi).wait_recv()
                state_copy(1, f, fi).wait_recv()
            consensus()
        else:
            def both_step(i, _):
                gather_time(i)
                forward_time(it, i)
                return 0

            lax.fori_loop(0, Q, both_step, 0)

        def backward_step(i, _):
            backward_time(it, i)
            return 0

        lax.fori_loop(0, Q, backward_step, 0)

        for h in range(2):
            scatter_half(it, h)
        for h in range(2):
            grad = gout[it, h, z]
            for v in column_others:
                go_copy(it, h, v, z).wait_recv()
                grad = grad + gin[it, h, v]
            for d in range(nd):
                de[it, fi, :, d * S + h * half:d * S + (h + 1) * half] = grad[:, d * half:(d + 1) * half]
        descent = de[it, fi] + du[fi] + rho[...] * (jn[fi] - fit[fi])
        de[it, fi] = descent
        squares = descent * descent
        total = squares[:, 0:128]
        for lo in range(128, L, 128):
            total = total + squares[:, lo:lo + 128]
        sq[it, q] = total
        last = it + 1 == ITERS
        if not last:
            for v in column_others:
                zd_copy(it, z, v).start()
        for f in freq_others:
            de_copy(it, fi, f).start()
        for to in plane_next:
            sq_copy(it, to).start()
        sq_all(it).wait_recv()
        sqs[it, fi * Z + z] = jnp.sum(sq[it], axis=0)
        each_other(lambda f, v: sums_copy(it, f, v).start())
        sums_all(it).wait_recv()
        for f in freq_others:
            de_copy(it, f, fi).wait_recv()
        if it == 0:
            for f in freq_others:
                state_copy(0, fi, f).wait_send()
                state_copy(1, fi, f).wait_send()
            for v in column_others:
                gz_copy(z, v).wait_send()
        scales = []
        for f in range(F):
            tile = jnp.sum(sqs[it, pl.ds(f * Z, Z)], axis=0)
            whole = jnp.sum(jnp.sum(tile, axis=1, keepdims=True), axis=0, keepdims=True)
            scale = jnp.sqrt(whole / (8.0 * K * S) + epsilon)
            scales.append(scale)
            jn[f] = jn[f] - step_size * de[it, f] / scale
        consensus()
        for f in range(F):
            du[f] = du[f] + rho[...] * (jn[f] - fit[f])
        if not last:
            own = scales[0]
            for f in range(1, F):
                own = jnp.where(fi == f, scales[f], own)
            gz[z] = jn[fi]
            for v in column_others:
                zd_copy(it, v, z).wait_recv()
                gz[v] = gz[v] - step_size * zde[it, v] / own

    jones_out[...] = jn[fi]
    dual_out[...] = du[fi]
    for to in plane_next:
        st_copy(q, to).wait_send()
        vis_copy(q, to).wait_send()
        coh_copy(q, to).wait_send()
        for it in range(ITERS):
            for u in range(Q):
                part_copy(it, u, q, to).wait_send()
    for it in range(ITERS):
        for v in column_others:
            go_copy(it, 0, z, v).wait_send()
            go_copy(it, 1, z, v).wait_send()
            if it + 1 < ITERS:
                zd_copy(it, z, v).wait_send()
        sq_all(it).wait_send()
        sums_all(it).wait_send()
        for f in freq_others:
            de_copy(it, fi, f).wait_send()


def body(visibilities, coherency, stations, jones, dual, cluster, rho_table):
    T = lax.axis_size("tm")
    F = lax.axis_size("freq")
    K, N = coherency.shape[3], coherency.shape[4]
    L = jones.shape[2]
    nd = K // T
    S = L // nd
    Z = max(ROWS // nd, math.gcd(T, 4))
    Q = T // Z
    D = Z * nd
    basis = poly_basis(F, min(3, F - 1))
    degrees = basis.shape[1]
    weight = np.float32(math.sqrt(S / (2.0 * T * N)))
    vmem = pl.BlockSpec(memory_space=pltpu.VMEM)
    smem = pl.BlockSpec(memory_space=pltpu.SMEM)
    anywhere = pl.BlockSpec(memory_space=pltpu.HBM)
    f32, bf16 = jnp.float32, jnp.bfloat16
    dma = pltpu.SemaphoreType.DMA
    jones_out, dual_out, poly = pl.pallas_call(
        functools.partial(kernel, T, F, Z, nd, S, K, N, basis, weight),
        out_shape=(
            jax.ShapeDtypeStruct((8, L), f32),
            jax.ShapeDtypeStruct((8, L), f32),
            jax.ShapeDtypeStruct((degrees, 8, L), f32),
        ),
        in_specs=[anywhere] * 5 + [smem] * 2,
        out_specs=(vmem, vmem, vmem),
        scratch_shapes=[
            pltpu.VMEM((Q, 8, N), f32),
            pltpu.VMEM((8, K, N), bf16),
            pltpu.VMEM((Q, 8 * D, N), bf16),
            pltpu.VMEM((Q, 8 * D, N), bf16),
            pltpu.VMEM((Q, 2, N), jnp.int32),
            pltpu.VMEM((Q, S, 2 * N), bf16),
            pltpu.VMEM((16 * D, S), bf16),
            pltpu.VMEM((2, S // 128, 8 * D, 128), f32),
            pltpu.VMEM((Z, 8, L), f32),
            pltpu.VMEM((ITERS, Z, 8, L), f32),
            pltpu.VMEM((Q, 2, 8 * D, N), f32),
            pltpu.VMEM((Q, 8 * D, N), f32),
            pltpu.VMEM((Q, 16 * D, 2 * N), bf16),
            pltpu.VMEM((ITERS, Q, 8, N), f32),
            pltpu.VMEM((ITERS, Q, Q, 8, N), f32),
            pltpu.VMEM((Q, 8, N), f32),
            pltpu.VMEM((2, S // 256, 8 * D, 128), f32),
            pltpu.VMEM((ITERS, 2, Z, 8, L // 2), f32),
            pltpu.VMEM((ITERS, 2, Z, 8, L // 2), f32),
            pltpu.VMEM((F, 8, L), f32),
            pltpu.VMEM((F, 8, L), f32),
            pltpu.VMEM((ITERS, F, 8, L), f32),
            pltpu.VMEM((F, 8, L), f32),
            pltpu.VMEM((8, L), f32),
            pltpu.VMEM((ITERS, Q, 8, 128), f32),
            pltpu.VMEM((ITERS, F * Z, 8, 128), f32),
            dma((5,)), dma((Q,)), dma((Q,)), dma((Q,)), dma((Q,)), dma((Q,)), dma((Q,)), dma((Z,)), dma((Z,)),
            dma((ITERS, Z)), dma((ITERS, Z)), dma((ITERS, Q, Q)), dma((ITERS, Q, Q)),
            dma((ITERS, 2, Z)), dma((ITERS, 2, Z)),
            dma((2, F)), dma((2, F)), dma((ITERS, F)), dma((ITERS, F)), dma((ITERS,)), dma((ITERS,)), dma((ITERS,)), dma((ITERS,)),
        ],
        compiler_params=pltpu.CompilerParams(
            collective_id=0, has_side_effects=True, vmem_limit_bytes=60 * 1024 * 1024),
        cost_estimate=pl.CostEstimate(flops=10**10, bytes_accessed=10**7, transcendentals=0),
    )(visibilities[0, 0], coherency[0, 0], stations[0], jones[0], dual[0], cluster, rho_table)
    return jones_out[None], dual_out[None], poly


def solution(mesh):
    return jax.shard_map(
        body,
        mesh=mesh,
        in_specs=(
            P("tm", "freq", None, None),
            P("tm", "freq", None, None, None),
            P("tm", None, None),
            P("freq", None, "tm"),
            P("freq", None, "tm"),
            P(),
            P(),
        ),
        out_specs=(P("freq", None, "tm"), P("freq", None, "tm"), P(None, None, "tm")),
        check_vma=False,
    )
```

```python
import functools
import math

import jax
import jax.numpy as jnp
import numpy as np
from jax import lax
from jax.experimental import pallas as pl
from jax.experimental.pallas import tpu as pltpu
from jax.sharding import PartitionSpec as P

ITERS = 2
MESH = pl.DeviceIdType.MESH
ROWS = 8

step_size = 0.5
epsilon = 1e-06


def poly_basis(channels, degrees):
    points = np.linspace(-1.0, 1.0, channels)
    columns = []
    for degree in range(degrees):
        column = points**degree
        for earlier in columns:
            column = column - np.dot(earlier, column) * earlier
        column = column / np.sqrt(np.dot(column, column))
        columns.append(column)
    return np.stack(columns, axis=1).astype(np.float32)


def split_entries(parts):
    return [[(parts[4 * i + 2 * j], parts[4 * i + 2 * j + 1]) for j in range(2)] for i in range(2)]


def join_entries(mat):
    return [part for row in mat for entry in row for part in entry]


def times_pair(a, b):
    return (a[0] * b[0] - a[1] * b[1], a[0] * b[1] + a[1] * b[0])


def times_conj(a, b):
    return (a[0] * b[0] + a[1] * b[1], a[1] * b[0] - a[0] * b[1])


def add_pairs(a, b):
    return (a[0] + b[0], a[1] + b[1])


def mat_mul(a, b):
    return [[add_pairs(times_pair(a[i][0], b[0][j]), times_pair(a[i][1], b[1][j])) for j in range(2)] for i in range(2)]


def mat_mul_right_h(a, b):
    return [[add_pairs(times_conj(a[i][0], b[j][0]), times_conj(a[i][1], b[j][1])) for j in range(2)] for i in range(2)]


def mat_mul_left_h(a, b):
    return [[add_pairs(times_conj(b[0][j], a[0][i]), times_conj(b[1][j], a[1][i])) for j in range(2)] for i in range(2)]


def kernel(
    T, F, Z, nd, S, K, N, basis, weight,
    vis_hbm, coh_hbm, st_hbm, jones_hbm, dual_hbm, cluster_ref, table_ref,
    jones_out, dual_out, poly_out,
    vis_all, coh_raw, coh_out, coh_in, st_all, oh, oht, tab, tabs, gz, zde, gp, abuf, xbuf, partial, part_in, res, acc, gout, gin,
    jn, du, de, fit, rho, sq, sqs,
    raw_sem, vi_ss, vi_rs, st_ss, st_rs, coh_ss, coh_rs, gz_ss, gz_rs, zd_ss, zd_rs, pa_ss, pa_rs, go_ss, go_rs,
    in_ss, in_rs, de_ss, de_rs, sq_ss, sq_rs, ss_ss, ss_rs,
):
    me = lax.axis_index("tm")
    fi = lax.axis_index("freq")
    Q = T // Z
    z, q = me // Q, lax.rem(me, Q)
    D = Z * nd
    tiles = D // ROWS
    g = ROWS // nd
    L = nd * S
    lane_tiles = S // 128
    half = S // 2
    degrees = basis.shape[1]

    def remote(src, dst, send, recv, to):
        return pltpu.make_async_remote_copy(
            src_ref=src, dst_ref=dst, send_sem=send, recv_sem=recv, device_id=to, device_id_type=MESH)

    def plane(u):
        return {"tm": z * Q + u}

    def column(v):
        return {"tm": v * Q + q}

    def st_copy(src, to):
        return remote(st_all.at[src], st_all.at[src], st_ss.at[to], st_rs.at[src], plane(to))

    def coh_copy(src, to):
        return remote(coh_out.at[to], coh_in.at[src], coh_ss.at[to], coh_rs.at[src], plane(to))

    def vis_copy(src, to):
        return remote(vis_all.at[src], vis_all.at[src], vi_ss.at[to], vi_rs.at[src], plane(to))

    def part_copy(it, u, src, to):
        return remote(
            partial.at[it, u], part_in.at[it, u, src], pa_ss.at[it, u], pa_rs.at[it, u], plane(to))

    def part_all(it, u):
        span = part_in.at[it, u, pl.ds(0, Q - 1)]
        return remote(span, span, pa_ss.at[it, u], pa_rs.at[it, u], plane(q))

    def gz_copy(src, to):
        return remote(gz.at[src], gz.at[src], gz_ss.at[to], gz_rs.at[src], column(to))

    def zd_copy(it, src, to):
        return remote(de.at[it, fi], zde.at[it, src], zd_ss.at[it, to], zd_rs.at[it, src], column(to))

    def go_copy(it, h, src, to):
        return remote(gout.at[it, h, to], gin.at[it, h, src], go_ss.at[it, h, to], go_rs.at[it, h, src], column(to))

    def state_copy(which, src, to):
        ref = (jn, du)[which]
        return remote(ref.at[src], ref.at[src], in_ss.at[which, to], in_rs.at[which, src], {"freq": to})

    def de_copy(it, src, to):
        return remote(de.at[it, src], de.at[it, src], de_ss.at[it, to], de_rs.at[it, src], {"freq": to})

    def sq_copy(it, to):
        return remote(sq.at[it, q], sq.at[it, q], sq_ss.at[it], sq_rs.at[it], plane(to))

    def sq_all(it):
        span = sq.at[it, pl.ds(0, Q - 1)]
        return remote(span, span, sq_ss.at[it], sq_rs.at[it], plane(q))

    def sums_copy(it, to_f, to_v):
        mine = fi * Z + z
        return remote(
            sqs.at[it, mine], sqs.at[it, mine], ss_ss.at[it], ss_rs.at[it], {"tm": to_v * Q + q, "freq": to_f})

    def sums_all(it):
        span = sqs.at[it, pl.ds(0, F * Z - 1)]
        return remote(span, span, ss_ss.at[it], ss_rs.at[it], {"tm": me, "freq": fi})

    def each_other(fn):
        def one(o, _):
            other = lax.rem(fi * Z + z + o, F * Z)
            fn(other // Z, lax.rem(other, Z))
            return 0
        lax.fori_loop(1, F * Z, one, 0)

    plane_next = [lax.rem(q + o, Q) for o in range(1, Q)]
    plane_from = [lax.rem(q - o + Q, Q) for o in range(1, Q)]
    column_others = [lax.rem(z + o, Z) for o in range(1, Z)]
    freq_others = [lax.rem(fi + o, F) for o in range(1, F)]

    jones_in = pltpu.make_async_copy(jones_hbm, jn.at[fi], raw_sem.at[0])
    st_in = pltpu.make_async_copy(st_hbm, st_all.at[q], raw_sem.at[1])
    raw = pltpu.make_async_copy(coh_hbm, coh_raw, raw_sem.at[2])
    dual_in = pltpu.make_async_copy(dual_hbm, du.at[fi], raw_sem.at[3])
    vis_in = pltpu.make_async_copy(vis_hbm, vis_all.at[q], raw_sem.at[4])
    for copy in (jones_in, st_in, raw, dual_in, vis_in):
        copy.start()
    barrier = pltpu.get_barrier_semaphore()

    for u in plane_next:
        pl.semaphore_signal(barrier, inc=1, device_id=plane(u), device_id_type=MESH)
    each_other(lambda f, v: pl.semaphore_signal(
        barrier, inc=1, device_id={"tm": v * Q + q, "freq": f}, device_id_type=MESH))
    jones_in.wait()
    gz[z] = jn[fi]
    st_in.wait()
    for d in range(nd):
        value = table_ref[cluster_ref[me * nd + d]]
        rho[:, d * S:(d + 1) * S] = jnp.full((ROWS, S), value, jnp.float32)
    pl.semaphore_wait(barrier, Q - 1 + F * Z - 1)

    for to in plane_next:
        st_copy(q, to).start()
    for to in column_others:
        gz_copy(z, to).start()
    raw.wait()

    slot = lax.broadcasted_iota(jnp.int32, (ROWS, N), 0) // nd
    for c in range(8):
        full = coh_raw[c].astype(jnp.float32)
        for u in range(Q):
            rows = []
            for m in range(tiles):
                out = None
                for s in range(g):
                    unit = (m * g + s) * Q + u
                    tile = full[8 * (unit // g):8 * (unit // g) + 8, :]
                    shift = ((s - unit % g) % g) * nd
                    if shift:
                        tile = pltpu.roll(tile, shift, 0)
                    out = tile if s == 0 else jnp.where(slot == s, tile, out)
                rows.append(out)
            block = rows[0] if tiles == 1 else jnp.concatenate(rows, axis=0)
            coh_out[u, c * D:(c + 1) * D, :] = block.astype(jnp.bfloat16)
    for to in plane_next:
        coh_copy(q, to).start()
    coh_in[q] = coh_out[q]
    dual_in.wait()
    vis_in.wait()
    for to in plane_next:
        vis_copy(q, to).start()
    for to in freq_others:
        state_copy(0, fi, to).start()
        state_copy(1, fi, to).start()

    def build(i, _):
        u = lax.rem(q - i + Q, Q)

        @pl.when(u != q)
        def _():
            st_copy(u, q).wait_recv()
        pair = jnp.concatenate([st_all[u]] * (ROWS // 2), axis=0).astype(jnp.float32)
        turned = jnp.transpose(pair)
        for e in range(2):
            for lo in range(0, N, 64):
                ids = lax.broadcasted_iota(jnp.int32, (64, S), 1).astype(jnp.float32)
                oht[u, e * N + lo:e * N + lo + 64, :] = jnp.where(
                    ids == turned[lo:lo + 64, e:e + 1], 1.0, 0.0).astype(jnp.bfloat16)
            row = st_all[u, e:e + 1, :]
            for lo in range(0, S, 64):
                ids = lax.broadcasted_iota(jnp.int32, (64, N), 0) + lo
                oh[u, lo:lo + 64, e * N:(e + 1) * N] = jnp.where(ids == row, 1.0, 0.0).astype(jnp.bfloat16)
        return 0

    lax.fori_loop(0, Q, build, 0)

    def set_table():
        for v in range(Z):
            now = gz[v]
            for d in range(nd):
                piece = now[:, d * S:(d + 1) * S]
                high = piece.astype(jnp.bfloat16).astype(jnp.float32)
                low = piece - high
                for k in range(lane_tiles):
                    lanes = slice(k * 128, (k + 1) * 128)
                    tabs[0, k, pl.ds(v * nd + d, 8, stride=D), :] = high[:, lanes]
                    tabs[1, k, pl.ds(v * nd + d, 8, stride=D), :] = low[:, lanes]
        for h in range(2):
            for k in range(lane_tiles):
                tab[h * 8 * D:(h + 1) * 8 * D, k * 128:(k + 1) * 128] = tabs[h, k].astype(jnp.bfloat16)

    def gather_time(u):
        for e in range(2):
            got = jnp.dot(tab[...], oh[u, :, e * N:(e + 1) * N], preferred_element_type=jnp.float32)
            gp[u, e] = got[:8 * D] + got[8 * D:]

    def tile_rows(c, m):
        return slice(c * D + m * ROWS, c * D + (m + 1) * ROWS)

    def sky_tiles(u, lanes):
        sky = [coh_in[u, c * D:(c + 1) * D, lanes].astype(jnp.float32) for c in range(8)]
        return [split_entries([part[m * ROWS:(m + 1) * ROWS] for part in sky]) for m in range(tiles)]

    def forward_time(it, u):
        for lo in range(0, N, 128):
            lanes = slice(lo, lo + 128)
            sky = sky_tiles(u, lanes)
            sums = None
            for m in range(tiles):
                first = split_entries([gp[u, 0, tile_rows(c, m), lanes] for c in range(8)])
                second = split_entries([gp[u, 1, tile_rows(c, m), lanes] for c in range(8)])
                prod = mat_mul(first, sky[m])
                for c, part in enumerate(join_entries(prod)):
                    abuf[u, tile_rows(c, m), lanes] = part
                model = join_entries(mat_mul_right_h(prod, second))
                sums = model if sums is None else [x + y for x, y in zip(sums, model)]
            for c in range(8):
                partial[it, u, c:c + 1, lanes] = jnp.sum(sums[c], axis=0, keepdims=True)

        for to in plane_next:
            part_copy(it, u, q, to).start()

    def backward_time(it, u):
        if it == 0:
            @pl.when(u != q)
            def _():
                vis_copy(u, q).wait_recv()
        model = partial[it, u]
        part_all(it, u).wait_recv()
        for src in plane_from:
            model = model + part_in[it, u, src]
        res[u] = weight * (model - vis_all[u])
        for lo in range(0, N, 128):
            lanes = slice(lo, lo + 128)
            sky = sky_tiles(u, lanes)
            resid = split_entries([
                jnp.broadcast_to(res[u, c:c + 1, lanes], (ROWS, 128)) for c in range(8)])
            grads = [[None] * (8 * tiles), [None] * (8 * tiles)]
            for m in range(tiles):
                prod = split_entries([abuf[u, tile_rows(c, m), lanes] for c in range(8)])
                second = split_entries([gp[u, 1, tile_rows(c, m), lanes] for c in range(8)])
                first_grad = join_entries(mat_mul(resid, mat_mul_right_h(second, sky[m])))
                second_grad = join_entries(mat_mul_left_h(resid, prod))
                for c in range(8):
                    grads[0][c * tiles + m] = first_grad[c]
                    grads[1][c * tiles + m] = second_grad[c]
            for e in range(2):
                for pair in range(4 * tiles):
                    both = jnp.concatenate(grads[e][2 * pair:2 * pair + 2], axis=0)
                    high = both.astype(jnp.bfloat16)
                    low = (both - high.astype(jnp.float32)).astype(jnp.bfloat16)
                    here = slice(e * N + lo, e * N + lo + 128)
                    xbuf[u, 16 * pair:16 * pair + 16, here] = high
                    xbuf[u, 8 * D + 16 * pair:8 * D + 16 * pair + 16, here] = low

    def scatter_half(it, h):
        def add_time(u, total):
            return total + jnp.dot(
                xbuf[u], oht[u, :, h * half:(h + 1) * half], preferred_element_type=jnp.float32)

        total = lax.fori_loop(0, Q, add_time, jnp.zeros((16 * D, half), jnp.float32))
        total = total[:8 * D] + total[8 * D:]
        for k in range(half // 128):
            acc[h, k] = total[:, k * 128:(k + 1) * 128]
        for v in range(Z):
            for d in range(nd):
                for k in range(half // 128):
                    gout[it, h, v, :, d * half + k * 128:d * half + (k + 1) * 128] = (
                        acc[h, k, pl.ds(v * nd + d, 8, stride=D), :])
        for v in column_others:
            go_copy(it, h, z, v).start()

    def consensus():
        sums = [jn[f] + du[f] / rho[...] for f in range(F)]
        for j in range(degrees):
            total = None
            for f in range(F):
                term = float(basis[f, j]) * sums[f]
                total = term if total is None else total + term
            poly_out[j] = total
        for f in range(F):
            total = None
            for j in range(degrees):
                term = float(basis[f, j]) * poly_out[j]
                total = term if total is None else total + term
            fit[f] = total

    for v in column_others:
        gz_copy(v, z).wait_recv()

    for it in range(ITERS):
        set_table()
        if it == 0:
            def gather_step(i, _):
                gather_time(i)
                return 0

            def forward_step(i, _):
                @pl.when(i != q)
                def _():
                    coh_copy(i, q).wait_recv()
                forward_time(it, i)
                return 0

            lax.fori_loop(0, Q, gather_step, 0)
            lax.fori_loop(0, Q, forward_step, 0)
            for f in freq_others:
                state_copy(0, f, fi).wait_recv()
                state_copy(1, f, fi).wait_recv()
            consensus()
        else:
            def both_step(i, _):
                gather_time(i)
                forward_time(it, i)
                return 0

            lax.fori_loop(0, Q, both_step, 0)

        def backward_step(i, _):
            backward_time(it, i)
            return 0

        lax.fori_loop(0, Q, backward_step, 0)

        for h in range(2):
            scatter_half(it, h)
        for h in range(2):
            grad = gout[it, h, z]
            for v in column_others:
                go_copy(it, h, v, z).wait_recv()
                grad = grad + gin[it, h, v]
            for d in range(nd):
                de[it, fi, :, d * S + h * half:d * S + (h + 1) * half] = grad[:, d * half:(d + 1) * half]
        descent = de[it, fi] + du[fi] + rho[...] * (jn[fi] - fit[fi])
        de[it, fi] = descent
        squares = descent * descent
        total = squares[:, 0:128]
        for lo in range(128, L, 128):
            total = total + squares[:, lo:lo + 128]
        sq[it, q] = total
        last = it + 1 == ITERS
        if not last:
            for v in column_others:
                zd_copy(it, z, v).start()
        for f in freq_others:
            de_copy(it, fi, f).start()
        for to in plane_next:
            sq_copy(it, to).start()
        sq_all(it).wait_recv()
        sqs[it, fi * Z + z] = jnp.sum(sq[it], axis=0)
        each_other(lambda f, v: sums_copy(it, f, v).start())
        sums_all(it).wait_recv()
        for f in freq_others:
            de_copy(it, f, fi).wait_recv()
        if it == 0:
            for f in freq_others:
                state_copy(0, fi, f).wait_send()
                state_copy(1, fi, f).wait_send()
            for v in column_others:
                gz_copy(z, v).wait_send()
        scales = []
        for f in range(F):
            tile = jnp.sum(sqs[it, pl.ds(f * Z, Z)], axis=0)
            whole = jnp.sum(jnp.sum(tile, axis=1, keepdims=True), axis=0, keepdims=True)
            scale = jnp.sqrt(whole / (8.0 * K * S) + epsilon)
            scales.append(scale)
            jn[f] = jn[f] - step_size * de[it, f] / scale
        consensus()
        for f in range(F):
            du[f] = du[f] + rho[...] * (jn[f] - fit[f])
        if not last:
            own = scales[0]
            for f in range(1, F):
                own = jnp.where(fi == f, scales[f], own)
            gz[z] = jn[fi]
            for v in column_others:
                zd_copy(it, v, z).wait_recv()
                gz[v] = gz[v] - step_size * zde[it, v] / own

    jones_out[...] = jn[fi]
    dual_out[...] = du[fi]
    for to in plane_next:
        st_copy(q, to).wait_send()
        vis_copy(q, to).wait_send()
        coh_copy(q, to).wait_send()
    for it in range(ITERS):
        for v in column_others:
            go_copy(it, 0, z, v).wait_send()
            go_copy(it, 1, z, v).wait_send()
            if it + 1 < ITERS:
                zd_copy(it, z, v).wait_send()
        for u in range(Q):
            part_all(it, u).wait_send()
        sq_all(it).wait_send()
        sums_all(it).wait_send()
        for f in freq_others:
            de_copy(it, fi, f).wait_send()


def body(visibilities, coherency, stations, jones, dual, cluster, rho_table):
    T = lax.axis_size("tm")
    F = lax.axis_size("freq")
    K, N = coherency.shape[3], coherency.shape[4]
    L = jones.shape[2]
    nd = K // T
    S = L // nd
    Z = max(ROWS // nd, math.gcd(T, 4))
    Q = T // Z
    D = Z * nd
    basis = poly_basis(F, min(3, F - 1))
    degrees = basis.shape[1]
    weight = np.float32(math.sqrt(S / (2.0 * T * N)))
    vmem = pl.BlockSpec(memory_space=pltpu.VMEM)
    smem = pl.BlockSpec(memory_space=pltpu.SMEM)
    anywhere = pl.BlockSpec(memory_space=pltpu.HBM)
    f32, bf16 = jnp.float32, jnp.bfloat16
    dma = pltpu.SemaphoreType.DMA
    jones_out, dual_out, poly = pl.pallas_call(
        functools.partial(kernel, T, F, Z, nd, S, K, N, basis, weight),
        out_shape=(
            jax.ShapeDtypeStruct((8, L), f32),
            jax.ShapeDtypeStruct((8, L), f32),
            jax.ShapeDtypeStruct((degrees, 8, L), f32),
        ),
        in_specs=[anywhere] * 5 + [smem] * 2,
        out_specs=(vmem, vmem, vmem),
        scratch_shapes=[
            pltpu.VMEM((Q, 8, N), f32),
            pltpu.VMEM((8, K, N), bf16),
            pltpu.VMEM((Q, 8 * D, N), bf16),
            pltpu.VMEM((Q, 8 * D, N), bf16),
            pltpu.VMEM((Q, 2, N), jnp.int32),
            pltpu.VMEM((Q, S, 2 * N), bf16),
            pltpu.VMEM((Q, 2 * N, S), bf16),
            pltpu.VMEM((16 * D, S), bf16),
            pltpu.VMEM((2, S // 128, 8 * D, 128), f32),
            pltpu.VMEM((Z, 8, L), f32),
            pltpu.VMEM((ITERS, Z, 8, L), f32),
            pltpu.VMEM((Q, 2, 8 * D, N), f32),
            pltpu.VMEM((Q, 8 * D, N), f32),
            pltpu.VMEM((Q, 16 * D, 2 * N), bf16),
            pltpu.VMEM((ITERS, Q, 8, N), f32),
            pltpu.VMEM((ITERS, Q, Q, 8, N), f32),
            pltpu.VMEM((Q, 8, N), f32),
            pltpu.VMEM((2, S // 256, 8 * D, 128), f32),
            pltpu.VMEM((ITERS, 2, Z, 8, L // 2), f32),
            pltpu.VMEM((ITERS, 2, Z, 8, L // 2), f32),
            pltpu.VMEM((F, 8, L), f32),
            pltpu.VMEM((F, 8, L), f32),
            pltpu.VMEM((ITERS, F, 8, L), f32),
            pltpu.VMEM((F, 8, L), f32),
            pltpu.VMEM((8, L), f32),
            pltpu.VMEM((ITERS, Q, 8, 128), f32),
            pltpu.VMEM((ITERS, F * Z, 8, 128), f32),
            dma((5,)), dma((Q,)), dma((Q,)), dma((Q,)), dma((Q,)), dma((Q,)), dma((Q,)), dma((Z,)), dma((Z,)),
            dma((ITERS, Z)), dma((ITERS, Z)), dma((ITERS, Q)), dma((ITERS, Q)),
            dma((ITERS, 2, Z)), dma((ITERS, 2, Z)),
            dma((2, F)), dma((2, F)), dma((ITERS, F)), dma((ITERS, F)), dma((ITERS,)), dma((ITERS,)), dma((ITERS,)), dma((ITERS,)),
        ],
        compiler_params=pltpu.CompilerParams(
            collective_id=0, has_side_effects=True, vmem_limit_bytes=60 * 1024 * 1024),
        cost_estimate=pl.CostEstimate(flops=10**10, bytes_accessed=10**7, transcendentals=0),
    )(visibilities[0, 0], coherency[0, 0], stations[0], jones[0], dual[0], cluster, rho_table)
    return jones_out[None], dual_out[None], poly


def solution(mesh):
    return jax.shard_map(
        body,
        mesh=mesh,
        in_specs=(
            P("tm", "freq", None, None),
            P("tm", "freq", None, None, None),
            P("tm", None, None),
            P("freq", None, "tm"),
            P("freq", None, "tm"),
            P(),
            P(),
        ),
        out_specs=(P("freq", None, "tm"), P("freq", None, "tm"), P(None, None, "tm")),
        check_vma=False,
    )
```

```python
import functools
import math

import jax
import jax.numpy as jnp
import numpy as np
from jax import lax
from jax.experimental import pallas as pl
from jax.experimental.pallas import tpu as pltpu
from jax.sharding import PartitionSpec as P

ITERS = 2
MESH = pl.DeviceIdType.MESH
ROWS = 8

step_size = 0.5
epsilon = 1e-06


def poly_basis(channels, degrees):
    points = np.linspace(-1.0, 1.0, channels)
    columns = []
    for degree in range(degrees):
        column = points**degree
        for earlier in columns:
            column = column - np.dot(earlier, column) * earlier
        column = column / np.sqrt(np.dot(column, column))
        columns.append(column)
    return np.stack(columns, axis=1).astype(np.float32)


def split_entries(parts):
    return [[(parts[4 * i + 2 * j], parts[4 * i + 2 * j + 1]) for j in range(2)] for i in range(2)]


def join_entries(mat):
    return [part for row in mat for entry in row for part in entry]


def times_pair(a, b):
    return (a[0] * b[0] - a[1] * b[1], a[0] * b[1] + a[1] * b[0])


def times_conj(a, b):
    return (a[0] * b[0] + a[1] * b[1], a[1] * b[0] - a[0] * b[1])


def add_pairs(a, b):
    return (a[0] + b[0], a[1] + b[1])


def mat_mul(a, b):
    return [[add_pairs(times_pair(a[i][0], b[0][j]), times_pair(a[i][1], b[1][j])) for j in range(2)] for i in range(2)]


def mat_mul_right_h(a, b):
    return [[add_pairs(times_conj(a[i][0], b[j][0]), times_conj(a[i][1], b[j][1])) for j in range(2)] for i in range(2)]


def mat_mul_left_h(a, b):
    return [[add_pairs(times_conj(b[0][j], a[0][i]), times_conj(b[1][j], a[1][i])) for j in range(2)] for i in range(2)]


def kernel(
    T, F, Z, nd, S, K, N, basis, weight,
    vis_hbm, coh_hbm, st_hbm, jones_hbm, dual_hbm, cluster_ref, table_ref,
    outs,
    vis_all, coh_raw, coh_out, coh_in, st_all, oh, oht, tab, tabs, gz, zde, gp, abuf, xbuf, partial, part_in, res, acc, gout, gin,
    jn, du, de, fit, rho, pol, sq, sqs,
    raw_sem, vi_ss, vi_rs, st_ss, st_rs, coh_ss, coh_rs, gz_ss, gz_rs, zd_ss, zd_rs, pa_ss, pa_rs, go_ss, go_rs,
    in_ss, in_rs, de_ss, de_rs, sq_ss, sq_rs, ss_ss, ss_rs,
):
    me = lax.axis_index("tm")
    fi = lax.axis_index("freq")
    Q = T // Z
    z, q = me // Q, lax.rem(me, Q)
    D = Z * nd
    tiles = D // ROWS
    g = ROWS // nd
    L = nd * S
    lane_tiles = S // 128
    half = S // 2
    degrees = basis.shape[1]

    def remote(src, dst, send, recv, to):
        return pltpu.make_async_remote_copy(
            src_ref=src, dst_ref=dst, send_sem=send, recv_sem=recv, device_id=to, device_id_type=MESH)

    def plane(u):
        return {"tm": z * Q + u}

    def column(v):
        return {"tm": v * Q + q}

    def st_copy(src, to):
        return remote(st_all.at[src], st_all.at[src], st_ss.at[to], st_rs.at[src], plane(to))

    def coh_copy(src, to):
        return remote(coh_out.at[to], coh_in.at[src], coh_ss.at[to], coh_rs.at[src], plane(to))

    def vis_copy(src, to):
        return remote(vis_all.at[src], vis_all.at[src], vi_ss.at[to], vi_rs.at[src], plane(to))

    def part_copy(it, u, src, to):
        return remote(
            partial.at[it, u], part_in.at[it, u, src], pa_ss.at[it, u], pa_rs.at[it, u], plane(to))

    def part_all(it, u):
        span = part_in.at[it, u, pl.ds(0, Q - 1)]
        return remote(span, span, pa_ss.at[it, u], pa_rs.at[it, u], plane(q))

    def gz_copy(src, to):
        return remote(gz.at[src], gz.at[src], gz_ss.at[to], gz_rs.at[src], column(to))

    def zd_copy(it, src, to):
        return remote(de.at[it, fi], zde.at[it, src], zd_ss.at[it, to], zd_rs.at[it, src], column(to))

    def go_copy(it, h, src, to):
        return remote(gout.at[it, h, to], gin.at[it, h, src], go_ss.at[it, h, to], go_rs.at[it, h, src], column(to))

    def state_copy(which, src, to):
        ref = (jn, du)[which]
        return remote(ref.at[src], ref.at[src], in_ss.at[which, to], in_rs.at[which, src], {"freq": to})

    def de_copy(it, src, to):
        return remote(de.at[it, src], de.at[it, src], de_ss.at[it, to], de_rs.at[it, src], {"freq": to})

    def sq_copy(it, to):
        return remote(sq.at[it, q], sq.at[it, q], sq_ss.at[it], sq_rs.at[it], plane(to))

    def sq_all(it):
        span = sq.at[it, pl.ds(0, Q - 1)]
        return remote(span, span, sq_ss.at[it], sq_rs.at[it], plane(q))

    def sums_copy(it, to_f, to_v):
        mine = fi * Z + z
        return remote(
            sqs.at[it, mine], sqs.at[it, mine], ss_ss.at[it], ss_rs.at[it], {"tm": to_v * Q + q, "freq": to_f})

    def sums_all(it):
        span = sqs.at[it, pl.ds(0, F * Z - 1)]
        return remote(span, span, ss_ss.at[it], ss_rs.at[it], {"tm": me, "freq": fi})

    def each_other(fn):
        def one(o, _):
            other = lax.rem(fi * Z + z + o, F * Z)
            fn(other // Z, lax.rem(other, Z))
            return 0
        lax.fori_loop(1, F * Z, one, 0)

    plane_next = [lax.rem(q + o, Q) for o in range(1, Q)]
    plane_from = [lax.rem(q - o + Q, Q) for o in range(1, Q)]
    column_others = [lax.rem(z + o, Z) for o in range(1, Z)]
    freq_others = [lax.rem(fi + o, F) for o in range(1, F)]

    jones_in = pltpu.make_async_copy(jones_hbm, jn.at[fi], raw_sem.at[0])
    st_in = pltpu.make_async_copy(st_hbm, st_all.at[q], raw_sem.at[1])
    raw = pltpu.make_async_copy(coh_hbm, coh_raw, raw_sem.at[2])
    dual_in = pltpu.make_async_copy(dual_hbm, du.at[fi], raw_sem.at[3])
    vis_in = pltpu.make_async_copy(vis_hbm, vis_all.at[q], raw_sem.at[4])
    for copy in (jones_in, st_in, raw, dual_in, vis_in):
        copy.start()
    barrier = pltpu.get_barrier_semaphore()

    for u in plane_next:
        pl.semaphore_signal(barrier, inc=1, device_id=plane(u), device_id_type=MESH)
    each_other(lambda f, v: pl.semaphore_signal(
        barrier, inc=1, device_id={"tm": v * Q + q, "freq": f}, device_id_type=MESH))
    jones_in.wait()
    gz[z] = jn[fi]
    st_in.wait()
    for d in range(nd):
        value = table_ref[cluster_ref[me * nd + d]]
        rho[:, d * S:(d + 1) * S] = jnp.full((ROWS, S), value, jnp.float32)
    pl.semaphore_wait(barrier, Q - 1 + F * Z - 1)

    for to in plane_next:
        st_copy(q, to).start()
    for to in column_others:
        gz_copy(z, to).start()
    raw.wait()

    slot = lax.broadcasted_iota(jnp.int32, (ROWS, N), 0) // nd
    for c in range(8):
        full = coh_raw[c].astype(jnp.float32)
        for u in range(Q):
            rows = []
            for m in range(tiles):
                out = None
                for s in range(g):
                    unit = (m * g + s) * Q + u
                    tile = full[8 * (unit // g):8 * (unit // g) + 8, :]
                    shift = ((s - unit % g) % g) * nd
                    if shift:
                        tile = pltpu.roll(tile, shift, 0)
                    out = tile if s == 0 else jnp.where(slot == s, tile, out)
                rows.append(out)
            block = rows[0] if tiles == 1 else jnp.concatenate(rows, axis=0)
            coh_out[u, c * D:(c + 1) * D, :] = block.astype(jnp.bfloat16)
    for to in plane_next:
        coh_copy(q, to).start()
    coh_in[q] = coh_out[q]
    dual_in.wait()
    vis_in.wait()
    for to in plane_next:
        vis_copy(q, to).start()
    for to in freq_others:
        state_copy(0, fi, to).start()
        state_copy(1, fi, to).start()

    def build(i, _):
        u = lax.rem(q - i + Q, Q)

        @pl.when(u != q)
        def _():
            st_copy(u, q).wait_recv()
        pair = jnp.concatenate([st_all[u]] * (ROWS // 2), axis=0).astype(jnp.float32)
        turned = jnp.transpose(pair)
        for e in range(2):
            for lo in range(0, N, 64):
                ids = lax.broadcasted_iota(jnp.int32, (64, S), 1).astype(jnp.float32)
                oht[u, e * N + lo:e * N + lo + 64, :] = jnp.where(
                    ids == turned[lo:lo + 64, e:e + 1], 1.0, 0.0).astype(jnp.bfloat16)
            row = st_all[u, e:e + 1, :]
            for lo in range(0, S, 64):
                ids = lax.broadcasted_iota(jnp.int32, (64, N), 0) + lo
                oh[u, lo:lo + 64, e * N:(e + 1) * N] = jnp.where(ids == row, 1.0, 0.0).astype(jnp.bfloat16)
        return 0

    lax.fori_loop(0, Q, build, 0)

    def set_table():
        for v in range(Z):
            now = gz[v]
            for d in range(nd):
                piece = now[:, d * S:(d + 1) * S]
                high = piece.astype(jnp.bfloat16).astype(jnp.float32)
                low = piece - high
                for k in range(lane_tiles):
                    lanes = slice(k * 128, (k + 1) * 128)
                    tabs[0, k, pl.ds(v * nd + d, 8, stride=D), :] = high[:, lanes]
                    tabs[1, k, pl.ds(v * nd + d, 8, stride=D), :] = low[:, lanes]
        for h in range(2):
            for k in range(lane_tiles):
                tab[h * 8 * D:(h + 1) * 8 * D, k * 128:(k + 1) * 128] = tabs[h, k].astype(jnp.bfloat16)

    def gather_time(u):
        for e in range(2):
            got = jnp.dot(tab[...], oh[u, :, e * N:(e + 1) * N], preferred_element_type=jnp.float32)
            gp[u, e] = got[:8 * D] + got[8 * D:]

    def tile_rows(c, m):
        return slice(c * D + m * ROWS, c * D + (m + 1) * ROWS)

    def sky_tiles(u, lanes):
        sky = [coh_in[u, c * D:(c + 1) * D, lanes].astype(jnp.float32) for c in range(8)]
        return [split_entries([part[m * ROWS:(m + 1) * ROWS] for part in sky]) for m in range(tiles)]

    def forward_time(it, u):
        for lo in range(0, N, 128):
            lanes = slice(lo, lo + 128)
            sky = sky_tiles(u, lanes)
            sums = None
            for m in range(tiles):
                first = split_entries([gp[u, 0, tile_rows(c, m), lanes] for c in range(8)])
                second = split_entries([gp[u, 1, tile_rows(c, m), lanes] for c in range(8)])
                prod = mat_mul(first, sky[m])
                for c, part in enumerate(join_entries(prod)):
                    abuf[u, tile_rows(c, m), lanes] = part
                model = join_entries(mat_mul_right_h(prod, second))
                sums = model if sums is None else [x + y for x, y in zip(sums, model)]
            for c in range(8):
                partial[it, u, c:c + 1, lanes] = jnp.sum(sums[c], axis=0, keepdims=True)

        for to in plane_next:
            part_copy(it, u, q, to).start()

    def backward_time(it, u):
        if it == 0:
            @pl.when(u != q)
            def _():
                vis_copy(u, q).wait_recv()
        model = partial[it, u]
        part_all(it, u).wait_recv()
        for src in plane_from:
            model = model + part_in[it, u, src]
        res[u] = weight * (model - vis_all[u])
        for lo in range(0, N, 128):
            lanes = slice(lo, lo + 128)
            sky = sky_tiles(u, lanes)
            resid = split_entries([
                jnp.broadcast_to(res[u, c:c + 1, lanes], (ROWS, 128)) for c in range(8)])
            grads = [[None] * (8 * tiles), [None] * (8 * tiles)]
            for m in range(tiles):
                prod = split_entries([abuf[u, tile_rows(c, m), lanes] for c in range(8)])
                second = split_entries([gp[u, 1, tile_rows(c, m), lanes] for c in range(8)])
                first_grad = join_entries(mat_mul(resid, mat_mul_right_h(second, sky[m])))
                second_grad = join_entries(mat_mul_left_h(resid, prod))
                for c in range(8):
                    grads[0][c * tiles + m] = first_grad[c]
                    grads[1][c * tiles + m] = second_grad[c]
            for e in range(2):
                for pair in range(4 * tiles):
                    both = jnp.concatenate(grads[e][2 * pair:2 * pair + 2], axis=0)
                    high = both.astype(jnp.bfloat16)
                    low = (both - high.astype(jnp.float32)).astype(jnp.bfloat16)
                    here = slice(e * N + lo, e * N + lo + 128)
                    xbuf[u, 16 * pair:16 * pair + 16, here] = high
                    xbuf[u, 8 * D + 16 * pair:8 * D + 16 * pair + 16, here] = low

    def scatter_half(it, h):
        def add_time(u, total):
            return total + jnp.dot(
                xbuf[u], oht[u, :, h * half:(h + 1) * half], preferred_element_type=jnp.float32)

        total = lax.fori_loop(0, Q, add_time, jnp.zeros((16 * D, half), jnp.float32))
        total = total[:8 * D] + total[8 * D:]
        for k in range(half // 128):
            acc[h, k] = total[:, k * 128:(k + 1) * 128]
        for v in range(Z):
            for d in range(nd):
                for k in range(half // 128):
                    gout[it, h, v, :, d * half + k * 128:d * half + (k + 1) * 128] = (
                        acc[h, k, pl.ds(v * nd + d, 8, stride=D), :])
        for v in column_others:
            go_copy(it, h, z, v).start()

    def consensus(last=False):
        sums = [jn[f] + du[f] / rho[...] for f in range(F)]
        for j in range(degrees):
            total = None
            for f in range(F):
                term = float(basis[f, j]) * sums[f]
                if last and f == F - 1:
                    outs[4 + 2 * j] = total
                    outs[5 + 2 * j] = term
                total = term if total is None else total + term
            pol[j] = total
        for f in range(F):
            total = None
            for j in range(degrees):
                term = float(basis[f, j]) * pol[j]
                total = term if total is None else total + term
            fit[f] = total

    for v in column_others:
        gz_copy(v, z).wait_recv()

    for it in range(ITERS):
        set_table()
        if it == 0:
            def gather_step(i, _):
                gather_time(i)
                return 0

            def forward_step(i, _):
                @pl.when(i != q)
                def _():
                    coh_copy(i, q).wait_recv()
                forward_time(it, i)
                return 0

            lax.fori_loop(0, Q, gather_step, 0)
            lax.fori_loop(0, Q, forward_step, 0)
            for f in freq_others:
                state_copy(0, f, fi).wait_recv()
                state_copy(1, f, fi).wait_recv()
            consensus()
        else:
            def both_step(i, _):
                gather_time(i)
                forward_time(it, i)
                return 0

            lax.fori_loop(0, Q, both_step, 0)

        def backward_step(i, _):
            backward_time(it, i)
            return 0

        lax.fori_loop(0, Q, backward_step, 0)

        for h in range(2):
            scatter_half(it, h)
        for h in range(2):
            grad = gout[it, h, z]
            for v in column_others:
                go_copy(it, h, v, z).wait_recv()
                grad = grad + gin[it, h, v]
            for d in range(nd):
                de[it, fi, :, d * S + h * half:d * S + (h + 1) * half] = grad[:, d * half:(d + 1) * half]
        descent = de[it, fi] + du[fi] + rho[...] * (jn[fi] - fit[fi])
        de[it, fi] = descent
        squares = descent * descent
        total = squares[:, 0:128]
        for lo in range(128, L, 128):
            total = total + squares[:, lo:lo + 128]
        sq[it, q] = total
        last = it + 1 == ITERS
        if not last:
            for v in column_others:
                zd_copy(it, z, v).start()
        for f in freq_others:
            de_copy(it, fi, f).start()
        for to in plane_next:
            sq_copy(it, to).start()
        sq_all(it).wait_recv()
        sqs[it, fi * Z + z] = jnp.sum(sq[it], axis=0)
        each_other(lambda f, v: sums_copy(it, f, v).start())
        sums_all(it).wait_recv()
        for f in freq_others:
            de_copy(it, f, fi).wait_recv()
        if it == 0:
            for f in freq_others:
                state_copy(0, fi, f).wait_send()
                state_copy(1, fi, f).wait_send()
            for v in column_others:
                gz_copy(z, v).wait_send()
        if last:
            outs[0] = jn[fi]
            outs[2] = du[fi]
        scales = []
        for f in range(F):
            tile = jnp.sum(sqs[it, pl.ds(f * Z, Z)], axis=0)
            whole = jnp.sum(jnp.sum(tile, axis=1, keepdims=True), axis=0, keepdims=True)
            scale = jnp.sqrt(whole / (8.0 * K * S) + epsilon)
            scales.append(scale)
            jn[f] = jn[f] - step_size * de[it, f] / scale
        consensus(last)
        own = scales[0]
        for f in range(1, F):
            own = jnp.where(fi == f, scales[f], own)
        if last:
            outs[1] = step_size * de[it, fi] / own
            outs[3] = rho[...] * (jn[fi] - fit[fi])
        else:
            for f in range(F):
                du[f] = du[f] + rho[...] * (jn[f] - fit[f])
            gz[z] = jn[fi]
            for v in column_others:
                zd_copy(it, v, z).wait_recv()
                gz[v] = gz[v] - step_size * zde[it, v] / own

    for to in plane_next:
        st_copy(q, to).wait_send()
        vis_copy(q, to).wait_send()
        coh_copy(q, to).wait_send()
    for it in range(ITERS):
        for v in column_others:
            go_copy(it, 0, z, v).wait_send()
            go_copy(it, 1, z, v).wait_send()
            if it + 1 < ITERS:
                zd_copy(it, z, v).wait_send()
        for u in range(Q):
            part_all(it, u).wait_send()
        sq_all(it).wait_send()
        sums_all(it).wait_send()
        for f in freq_others:
            de_copy(it, fi, f).wait_send()


def body(visibilities, coherency, stations, jones, dual, cluster, rho_table):
    T = lax.axis_size("tm")
    F = lax.axis_size("freq")
    K, N = coherency.shape[3], coherency.shape[4]
    L = jones.shape[2]
    nd = K // T
    S = L // nd
    Z = max(ROWS // nd, math.gcd(T, 4))
    Q = T // Z
    D = Z * nd
    basis = poly_basis(F, min(3, F - 1))
    degrees = basis.shape[1]
    weight = np.float32(math.sqrt(S / (2.0 * T * N)))
    vmem = pl.BlockSpec(memory_space=pltpu.VMEM)
    smem = pl.BlockSpec(memory_space=pltpu.SMEM)
    anywhere = pl.BlockSpec(memory_space=pltpu.HBM)
    f32, bf16 = jnp.float32, jnp.bfloat16
    dma = pltpu.SemaphoreType.DMA
    outs = pl.pallas_call(
        functools.partial(kernel, T, F, Z, nd, S, K, N, basis, weight),
        out_shape=jax.ShapeDtypeStruct((4 + 2 * degrees, 8, L), f32),
        in_specs=[anywhere] * 5 + [smem] * 2,
        out_specs=vmem,
        scratch_shapes=[
            pltpu.VMEM((Q, 8, N), f32),
            pltpu.VMEM((8, K, N), bf16),
            pltpu.VMEM((Q, 8 * D, N), bf16),
            pltpu.VMEM((Q, 8 * D, N), bf16),
            pltpu.VMEM((Q, 2, N), jnp.int32),
            pltpu.VMEM((Q, S, 2 * N), bf16),
            pltpu.VMEM((Q, 2 * N, S), bf16),
            pltpu.VMEM((16 * D, S), bf16),
            pltpu.VMEM((2, S // 128, 8 * D, 128), f32),
            pltpu.VMEM((Z, 8, L), f32),
            pltpu.VMEM((ITERS, Z, 8, L), f32),
            pltpu.VMEM((Q, 2, 8 * D, N), f32),
            pltpu.VMEM((Q, 8 * D, N), f32),
            pltpu.VMEM((Q, 16 * D, 2 * N), bf16),
            pltpu.VMEM((ITERS, Q, 8, N), f32),
            pltpu.VMEM((ITERS, Q, Q, 8, N), f32),
            pltpu.VMEM((Q, 8, N), f32),
            pltpu.VMEM((2, S // 256, 8 * D, 128), f32),
            pltpu.VMEM((ITERS, 2, Z, 8, L // 2), f32),
            pltpu.VMEM((ITERS, 2, Z, 8, L // 2), f32),
            pltpu.VMEM((F, 8, L), f32),
            pltpu.VMEM((F, 8, L), f32),
            pltpu.VMEM((ITERS, F, 8, L), f32),
            pltpu.VMEM((F, 8, L), f32),
            pltpu.VMEM((8, L), f32),
            pltpu.VMEM((degrees, 8, L), f32),
            pltpu.VMEM((ITERS, Q, 8, 128), f32),
            pltpu.VMEM((ITERS, F * Z, 8, 128), f32),
            dma((5,)), dma((Q,)), dma((Q,)), dma((Q,)), dma((Q,)), dma((Q,)), dma((Q,)), dma((Z,)), dma((Z,)),
            dma((ITERS, Z)), dma((ITERS, Z)), dma((ITERS, Q)), dma((ITERS, Q)),
            dma((ITERS, 2, Z)), dma((ITERS, 2, Z)),
            dma((2, F)), dma((2, F)), dma((ITERS, F)), dma((ITERS, F)), dma((ITERS,)), dma((ITERS,)), dma((ITERS,)), dma((ITERS,)),
        ],
        compiler_params=pltpu.CompilerParams(
            collective_id=0, has_side_effects=True, vmem_limit_bytes=60 * 1024 * 1024),
        cost_estimate=pl.CostEstimate(flops=10**10, bytes_accessed=10**7, transcendentals=0),
    )(visibilities[0, 0], coherency[0, 0], stations[0], jones[0], dual[0], cluster, rho_table)
    return outs[0:1] - outs[1:2], outs[2:3] + outs[3:4], outs[4::2] + outs[5::2]


def solution(mesh):
    return jax.shard_map(
        body,
        mesh=mesh,
        in_specs=(
            P("tm", "freq", None, None),
            P("tm", "freq", None, None, None),
            P("tm", None, None),
            P("freq", None, "tm"),
            P("freq", None, "tm"),
            P(),
            P(),
        ),
        out_specs=(P("freq", None, "tm"), P("freq", None, "tm"), P(None, None, "tm")),
        check_vma=False,
    )
```
